256 devices in a mesh: leaf: 32 (over z, y), front: 8 (over x, core).
Axes of the slice: x: 4, y: 4, z: 8, core: 2. Of those that a mesh axis runs over, the one named last changes fastest.
Arguments:
- rhs_sub: float32 [131072, 64], P(('leaf', 'front')), may hold values from -6 to 6
- rhs_root: float32 [12288, 64], P(('leaf', 'front')), may hold values from -6 to 6
- factor_sub: bfloat16 [32, 4096, 4096], P('leaf', 'front'), may hold values from -0.09375 to 0.09375
- coupling: bfloat16 [32, 2048, 4096], P('leaf', None, 'front'), may hold values from -0.09375 to 0.09375
- update_rows: int32 [32, 2048], P('leaf'), may hold values from 0 to 12287, as said below
- factor_root: bfloat16 [12288, 12288], P(('leaf', 'front')), may hold values from -0.0546875 to 0.0546875
- mass_sub: float32 [131072], P(('leaf', 'front')), may hold values from 0.5 to 2
- mass_root: float32 [12288], P(('leaf', 'front')), may hold values from 0.5 to 2
- interface: bfloat16 [256, 256, 256], P(('leaf', 'front')), may hold values from -0.375 to 0.375
- basis_sub: bfloat16 [131072, 2048], P(('leaf', 'front')), may hold values from -0.046875 to 0.046875
- basis_root: bfloat16 [12288, 2048], P(('leaf', 'front')), may hold values from -0.046875 to 0.046875
Outputs:
- new_sub: float32 [131072, 64], P(('leaf', 'front'))
- new_root: float32 [12288, 64], P(('leaf', 'front'))
- gram: float32 [2048, 64], replicated
The draws below stay inside these ranges and needn't reach their ends.
Inputs may be any that keep to these rules, and one draw needn't show every extreme that they name: Each row of update_rows lists 2048 distinct root rows.
All inputs are finite; a program needn't handle non-finite values.
Results may differ from the reference program's by a relative error of at most 0.015.
Values may be sent and summed in bfloat16 or wider, within the bound.
A program may use at most 128 MiB of HBM per device.

```python
import jax
import jax.numpy as jnp
from jax import lax

NRHS = 64
SUBFRONT = 4096
ROOT = 12288
UPDATE = 2048
RIM = 256
BLOCKS = 32
GROUPS = 32
N_FRONT = 8


def draw_update_rows(key, part):
    key = jax.random.fold_in(key, 5)
    group_keys = jax.random.split(key, GROUPS)
    chosen = jax.vmap(lambda k: jax.random.permutation(k, ROOT)[:UPDATE])(group_keys)
    return chosen.astype(jnp.int32)


def block_levels(key, shape, cuts, smallest, largest):
    loudness = 1.0
    for position, blocks in cuts:
        steps = jax.random.uniform(jax.random.fold_in(jax.random.fold_in(key, 6), position), (blocks,), jnp.float32, smallest / len(cuts), largest / len(cuts))
        loudness = loudness * jnp.repeat(jnp.exp(steps), shape[position] // blocks).reshape((-1,) + (1,) * (len(shape) - 1 - position))
    return loudness


def noise(stream_key, dims, scale, limit, cuts=(), dtype=jnp.bfloat16):
    result = scale * jax.random.normal(stream_key, dims, jnp.float32)
    if cuts:
        result = result * block_levels(stream_key, dims, cuts, -0.22, 0.18)
    return jnp.clip(result, -limit, limit).astype(dtype)


def setup_inputs(seed: int = 0) -> dict:
    key_of = jax.random.split(jax.random.key(seed), 12)
    rhs_sub = noise(key_of[0], (GROUPS * SUBFRONT, NRHS), 1.0, 6.0, ((0, 256),), jnp.float32)
    rhs_root = noise(key_of[1], (ROOT, NRHS), 1.0, 6.0, ((0, 256),), jnp.float32)
    factor_sub = noise(key_of[2], (GROUPS, SUBFRONT, SUBFRONT), SUBFRONT ** -0.5, 0.09375, ((0, 32), (1, 8)))
    coupling = noise(key_of[3], (GROUPS, UPDATE, SUBFRONT), SUBFRONT ** -0.5, 0.09375, ((0, 32), (2, 8)))
    update_rows = draw_update_rows(jax.random.fold_in(key_of[11], 71), 0)
    factor_root = noise(key_of[5], (ROOT, ROOT), ROOT ** -0.5, 0.0546875, ((0, 256),))
    mass_sub = jnp.clip(0.5 + 1.5 * jax.random.uniform(key_of[6], (GROUPS * SUBFRONT,), jnp.float32) ** block_levels(key_of[6], (GROUPS * SUBFRONT,), ((0, 256),), -0.2, 0.2), 0.5, 2.0)
    mass_root = jnp.clip(0.5 + 1.5 * jax.random.uniform(key_of[7], (ROOT,), jnp.float32) ** block_levels(key_of[7], (ROOT,), ((0, 256),), -0.2, 0.2), 0.5, 2.0)
    interface = noise(key_of[8], (GROUPS * N_FRONT, RIM, RIM), RIM ** -0.5, 0.375, ((0, 256),))
    basis_sub = noise(key_of[9], (GROUPS * SUBFRONT, BLOCKS * NRHS), (8 * BLOCKS * NRHS) ** -0.5, 0.046875, ((0, 256),))
    basis_root = noise(key_of[10], (ROOT, BLOCKS * NRHS), (8 * BLOCKS * NRHS) ** -0.5, 0.046875, ((0, 256),))
    return dict(rhs_sub=rhs_sub, rhs_root=rhs_root, factor_sub=factor_sub, coupling=coupling, update_rows=update_rows, factor_root=factor_root, mass_sub=mass_sub, mass_root=mass_root, interface=interface, basis_sub=basis_sub, basis_root=basis_root)


def reference(rhs_sub, rhs_root, factor_sub, coupling, update_rows, factor_root, mass_sub, mass_root, interface, basis_sub, basis_root):
    lower_mask = jnp.arange(SUBFRONT)[None, :] <= jnp.arange(SUBFRONT)[:, None]
    rhs_low = rhs_sub.astype(jnp.bfloat16).reshape(GROUPS, SUBFRONT, NRHS)

    def forward_one(operands):
        masked = jnp.where(lower_mask, operands[0], jnp.zeros((), jnp.bfloat16))
        return jnp.dot(masked, operands[1], preferred_element_type=jnp.float32)

    y_sub = lax.map(forward_one, (factor_sub, rhs_low))
    y_low = y_sub.astype(jnp.bfloat16)
    update_terms = lax.map(lambda ops: jnp.dot(ops[0], ops[1], preferred_element_type=jnp.float32), (coupling, y_low))
    summed = jnp.zeros((ROOT, NRHS), jnp.float32).at[update_rows.reshape(-1)].add(update_terms.reshape(-1, NRHS))
    root_low = (rhs_root - summed).astype(jnp.bfloat16)
    root_mask = jnp.arange(ROOT)[None, :] <= jnp.arange(ROOT)[:, None]
    masked_root = jnp.where(root_mask, factor_root, jnp.zeros((), jnp.bfloat16))
    y_root = jnp.dot(masked_root, root_low, preferred_element_type=jnp.float32)
    x_root = jnp.dot(masked_root.T, y_root.astype(jnp.bfloat16), preferred_element_type=jnp.float32)
    x_root_low = x_root.astype(jnp.bfloat16)

    def pull_one(operands):
        picked = jnp.take(x_root_low, operands[1], axis=0)
        return jnp.dot(operands[0].T, picked, preferred_element_type=jnp.float32)

    t_sub = y_sub - lax.map(pull_one, (coupling, update_rows))
    t_low = t_sub.astype(jnp.bfloat16)

    def backward_one(operands):
        masked = jnp.where(lower_mask, operands[0], jnp.zeros((), jnp.bfloat16))
        return jnp.dot(masked.T, operands[1], preferred_element_type=jnp.float32)

    x_sub = lax.map(backward_one, (factor_sub, t_low))
    x_low = x_sub.astype(jnp.bfloat16)
    share = SUBFRONT // N_FRONT
    x_shares = x_low.reshape(GROUPS, N_FRONT, share, NRHS).astype(jnp.float32)
    below = x_shares[:, :, share - RIM:, :]
    above = x_shares[:, :, :RIM, :]
    blocks_f = interface.astype(jnp.float32).reshape(GROUPS, N_FRONT, RIM, RIM)
    previous = jnp.roll(below, 1, axis=0)
    first_add = jnp.einsum('gfij,gfjn->gfin', blocks_f, previous)
    back_terms = jnp.einsum('gfji,gfjn->gfin', blocks_f, above)
    last_add = jnp.roll(back_terms, -1, axis=0)
    mass_x = mass_sub.reshape(GROUPS, N_FRONT, share, 1) * x_sub.reshape(GROUPS, N_FRONT, share, NRHS)
    mass_x = mass_x.at[:, :, :RIM, :].add(first_add)
    mass_x = mass_x.at[:, :, share - RIM:, :].add(last_add)
    mass_root_x = mass_root[:, None] * x_root
    gram = jnp.dot(basis_sub.T, mass_x.reshape(-1, NRHS).astype(jnp.bfloat16), preferred_element_type=jnp.float32)
    gram = gram + jnp.dot(basis_root.T, mass_root_x.astype(jnp.bfloat16), preferred_element_type=jnp.float32)
    gram_low = gram.astype(jnp.bfloat16)
    new_sub = x_sub.reshape(-1, NRHS) - jnp.dot(basis_sub, gram_low, preferred_element_type=jnp.float32)
    new_root = x_root - jnp.dot(basis_root, gram_low, preferred_element_type=jnp.float32)
    return (new_sub, new_root, gram)
```

```python
import jax
import jax.numpy as jnp
from jax import lax
from jax.experimental import pallas as pl
from jax.experimental.pallas import tpu as pltpu
from jax.sharding import PartitionSpec as P

BF = jnp.bfloat16
F32 = jnp.float32
MESH = pl.DeviceIdType.MESH

N = 64
NF = 8
NY = 4
NZ = 8
SH = 512
SUB = NF * SH
UP = 2048
UPS = UP // NF
RR = 48
GR = NF * RR
SL = NY * GR
ROOT = NF * SL
RIM = 256
NB = 2048
NBS = NB // NF
PAD = 128

STAGES = 25


def dot(a, b):
    return jnp.dot(a, b, preferred_element_type=F32)


def dot_t(a, b):
    return lax.dot_general(a, b, (((1,), (1,)), ((), ())), preferred_element_type=F32)


def kernel(
    rhs_ref,
    rroot_ref,
    factor_hbm,
    coupling_hbm,
    rows_ref,
    froot_hbm,
    mass_ref,
    mroot_ref,
    iface_ref,
    basis_hbm,
    broot_hbm,
    new_sub_ref,
    new_root_ref,
    gram_ref,
    fac,
    cpl,
    onehot,
    frt,
    bas,
    brt,
    rhs_all,
    rr_send,
    rr_all,
    rr_sum,
    y_acc,
    up_send,
    up_recv,
    up_all,
    d_send,
    d_recv,
    d_zsend,
    d_zrecv,
    d_zall,
    d_all,
    yr_all,
    x_send,
    x_recv,
    x_zsend,
    x_zrecv,
    x_zall,
    x_all,
    xr_recv,
    pk_send,
    pk_recv,
    pk_all,
    xs_send,
    xs_recv,
    xs_acc,
    if_send,
    if_recv,
    g_send,
    g_recv,
    g_ysend,
    g_yrecv,
    g_zall,
    g_yall,
    g_all,
    ssem,
    rsem,
    lsem,
):
    g = lax.axis_index("leaf")
    f = lax.axis_index("front")
    z = lax.div(g, NY)
    y = lax.rem(g, NY)

    def dev_f(i):
        return (g, i)

    def dev_y(i):
        return (z * NY + i, f)

    def dev_z(i):
        return (i * NY + y, f)

    nxt = lax.rem(g + 1, NY * NZ)
    prv = lax.rem(g + NY * NZ - 1, NY * NZ)

    barrier = pltpu.get_barrier_semaphore()
    peers = [dev_f(lax.rem(f + k, NF)) for k in range(1, NF)]
    peers += [dev_y(lax.rem(y + k, NY)) for k in range(1, NY)]
    peers += [dev_z(lax.rem(z + k, NZ)) for k in range(1, NZ)]
    peers += [(nxt, f), (prv, f)]
    for dev in peers:
        pl.semaphore_signal(barrier, inc=1, device_id=dev, device_id_type=MESH)

    load_fac = pltpu.make_async_copy(factor_hbm, fac, lsem.at[0])
    load_cpl = pltpu.make_async_copy(coupling_hbm, cpl, lsem.at[1])
    load_bas = pltpu.make_async_copy(basis_hbm, bas, lsem.at[2])
    load_brt = pltpu.make_async_copy(broot_hbm, brt.at[pl.ds(0, RR)], lsem.at[3])
    load_frt = pltpu.make_async_copy(
        froot_hbm.at[:, pl.ds(pl.multiple_of(f * SL, 128), SL)],
        frt.at[pl.ds(pl.multiple_of(f * RR, 16), RR)],
        lsem.at[4],
    )
    load_fac.start()
    load_cpl.start()
    load_frt.start()
    load_bas.start()
    load_brt.start()

    sends = []

    def push(src, dst, stage, k, slot, dev, cond=None):
        copy = pltpu.make_async_remote_copy(
            src_ref=src,
            dst_ref=dst,
            send_sem=ssem.at[stage, k],
            recv_sem=rsem.at[stage, slot],
            device_id=dev,
            device_id_type=MESH,
        )
        if cond is None:
            copy.start()
        else:
            pl.when(cond)(copy.start)
        sends.append((copy, cond))

    def await_slot(buf, stage, slot):
        pltpu.make_async_remote_copy(
            src_ref=buf,
            dst_ref=buf,
            send_sem=ssem.at[stage, 0],
            recv_sem=rsem.at[stage, slot],
            device_id=(g, f),
            device_id_type=MESH,
        ).wait_recv()

    def await_ring(buf, stage, me, n):
        for k in range(1, n):
            p = lax.rem(me + n - k, n)
            await_slot(buf.at[p], stage, p)

    spot = lax.broadcasted_iota(jnp.int32, (PAD, GR), 0)
    lane = lax.broadcasted_iota(jnp.int32, (PAD, GR), 1)
    place = jnp.where((lane == spot + f * RR) & (spot < RR), 1.0, 0.0).astype(BF)
    rr_mine = dot(rroot_ref[...], place).astype(BF)
    rr_send[...] = rr_mine
    rr_all[f] = rr_mine

    pl.semaphore_wait(barrier, len(peers))

    for k in range(1, NF):
        p = lax.rem(f + k, NF)
        push(rhs_ref, rhs_all.at[f], 0, k, f, dev_f(p), f + k < NF)
    push(rr_send, rr_all.at[f], 1, 0, f, dev_f(z), f != z)
    for k in range(1, NF):
        p = lax.rem(f + k, NF)
        push(
            froot_hbm.at[:, pl.ds(pl.multiple_of(p * SL, 128), SL)],
            frt.at[pl.ds(pl.multiple_of(f * RR, 16), RR)],
            2,
            k,
            f,
            dev_f(p),
        )

    def hot(i, _):
        at = pl.multiple_of(i * 64, 64)
        ids = lax.broadcasted_iota(jnp.int32, (64, UP), 0) + (f * SL + i * 64)
        onehot[pl.ds(at, 64), :] = jnp.where(ids == rows_ref[...], 1.0, 0.0).astype(BF)
        return 0

    lax.fori_loop(0, SL // 64, hot, 0)

    load_fac.wait()
    mine = pl.ds(pl.multiple_of(f * SH, 128), SH)
    below = lax.broadcasted_iota(jnp.int32, (SH, SH), 1) <= lax.broadcasted_iota(
        jnp.int32, (SH, SH), 0
    )
    diag = jnp.where(below, fac[:, mine].astype(F32), 0.0).astype(BF)
    fac[:, mine] = diag
    y_acc[...] = dot_t(rhs_ref[...], diag)
    for k in range(1, NF):

        @pl.when(f >= k)
        def _(k=k):
            p = f - k
            await_slot(rhs_all.at[p], 0, p)
            cols = pl.ds(pl.multiple_of(p * SH, 128), SH)
            y_acc[...] += dot_t(rhs_all[p], fac[:, cols])

    y_low = y_acc[...].astype(BF)

    load_cpl.wait()
    for k in range(1, NF + 1):
        p = lax.rem(f + k, NF)
        rows = pl.ds(pl.multiple_of(p * UPS, 128), UPS)
        piece = dot_t(y_low, cpl[rows, :]).astype(BF)
        if k < NF:
            up_send[k] = piece
            push(up_send.at[k], up_recv.at[f], 3, k, f, dev_f(p))
        else:
            up_recv[f] = piece
    await_ring(up_recv, 3, f, NF)
    up_all[f] = sum(up_recv[j].astype(F32) for j in range(NF)).astype(BF)
    for k in range(1, NF):
        push(up_all.at[f], up_all.at[f], 4, k, f, dev_f(lax.rem(f + k, NF)))
    await_ring(up_all, 4, f, NF)

    def leaf_sum(chunk, own, send, recv, zsend, zrecv, zall, full, stage, early=None):
        for k in range(1, NY + 1):
            p = lax.rem(y + k, NY)
            piece = chunk(p)
            if k < NY:
                send[k] = piece.astype(BF)
                push(send.at[k], recv.at[y], stage, k, y, dev_y(p))
            else:
                recv[y] = piece.astype(BF)
        await_ring(recv, stage, y, NY)
        part = sum(recv[j].astype(F32) for j in range(NY))
        part = own(part)
        zsend[...] = part.reshape(NZ, N // NZ, GR)
        zrecv[z] = zsend[z]
        for k in range(1, NZ):
            p = lax.rem(z + k, NZ)
            push(zsend.at[p], zrecv.at[z], stage + 1, k, z, dev_z(p))
        await_ring(zrecv, stage + 1, z, NZ)
        zall[z] = sum(zrecv[j] for j in range(NZ))
        for k in range(1, NZ):
            push(zall.at[z], zall.at[z], stage + 2, k, z, dev_z(lax.rem(z + k, NZ)))
        await_ring(zall, stage + 2, z, NZ)
        full[y] = zall[...].reshape(N, GR).astype(BF)
        for k in range(1, NY):
            push(full.at[y], full.at[y], stage + 3, k, y, dev_y(lax.rem(y + k, NY)))
        if early is not None:
            early()
        await_ring(full, stage + 3, y, NY)
        return jnp.concatenate([full[j] for j in range(NY)], axis=1)

    up_low = jnp.concatenate([up_all[j] for j in range(NF)], axis=1)

    def scatter_chunk(q):
        return -dot_t(up_low, onehot[pl.ds(pl.multiple_of(q * GR, 128), GR), :])

    rr_sum[...] = jnp.zeros_like(rr_sum)

    @pl.when(f == z)
    def _():
        await_ring(rr_all, 1, f, NF)
        rr_sum[...] = sum(rr_all[j].astype(F32) for j in range(NF))

    b_low = leaf_sum(
        scatter_chunk,
        lambda part: part + rr_sum[...],
        d_send,
        d_recv,
        d_zsend,
        d_zrecv,
        d_zall,
        d_all,
        5,
    )

    load_frt.wait()
    for k in range(1, NF):
        p = lax.rem(f + NF - k, NF)
        await_slot(frt.at[pl.ds(pl.multiple_of(p * RR, 16), RR)], 2, p)
    for j in range(NF):
        rows = pl.ds(j * RR, RR)
        row_ids = lax.broadcasted_iota(jnp.int32, (RR, SL), 0) + (g * GR + j * RR)
        col_ids = lax.broadcasted_iota(jnp.int32, (RR, SL), 1) + f * SL
        kept = jnp.where(col_ids <= row_ids, frt[rows, :].astype(F32), 0.0)
        frt[rows, :] = kept.astype(BF)
    yr_all[f] = dot_t(b_low, frt[...]).astype(BF)
    for k in range(1, NF):
        push(yr_all.at[f], yr_all.at[f], 9, k, f, dev_f(lax.rem(f + k, NF)))
    await_ring(yr_all, 9, f, NF)
    yr_low = sum(yr_all[j].astype(F32) for j in range(NF)).astype(BF)

    def back_chunk(q):
        return dot(yr_low, frt[:, pl.ds(pl.multiple_of(q * GR, 128), GR)])

    def hand_block():
        @pl.when(f == z)
        def _():
            xr_recv[...] = x_all[y]

        for k in range(1, NF):
            push(x_all.at[y], xr_recv, 14, k, 0, dev_f(lax.rem(f + k, NF)), f == z)

    x_low = leaf_sum(
        back_chunk,
        lambda part: part,
        x_send,
        x_recv,
        x_zsend,
        x_zrecv,
        x_zall,
        x_all,
        10,
        hand_block,
    )

    for k in range(1, NF + 1):
        p = lax.rem(f + k, NF)
        cols = pl.ds(pl.multiple_of(p * UPS, 128), UPS)
        piece = dot(x_low, onehot[:, cols]).astype(BF)
        if k < NF:
            pk_send[k] = piece
            push(pk_send.at[k], pk_recv.at[f], 15, k, f, dev_f(p))
        else:
            pk_recv[f] = piece
    await_ring(pk_recv, 15, f, NF)
    pk_all[f] = sum(pk_recv[j].astype(F32) for j in range(NF)).astype(BF)
    for k in range(1, NF):
        push(pk_all.at[f], pk_all.at[f], 16, k, f, dev_f(lax.rem(f + k, NF)))
    await_ring(pk_all, 16, f, NF)
    for j in range(NF):
        y_acc[...] -= dot(pk_all[j], cpl[pl.ds(j * UPS, UPS), :])
    t_low = y_acc[...].astype(BF)

    for k in range(1, NF):

        @pl.when(f >= k)
        def _(k=k):
            cols = pl.ds(pl.multiple_of((f - k) * SH, 128), SH)
            xs_send[k] = dot(t_low, fac[:, cols]).astype(BF)

        push(xs_send.at[k], xs_recv.at[f], 17, k, f, dev_f(lax.rem(f + NF - k, NF)), f >= k)
    xs_acc[...] = dot(t_low, fac[:, mine])
    for k in range(1, NF):

        @pl.when(f + k < NF)
        def _(k=k):
            await_slot(xs_recv.at[f + k], 17, f + k)
            xs_acc[...] += xs_recv[f + k].astype(F32)

    xs_low = xs_acc[...].astype(BF)
    if_send[0] = xs_low[:, SH - RIM :]
    push(if_send.at[0], if_recv.at[0], 18, 0, 0, (nxt, f))
    if_send[1] = dot(xs_low[:, :RIM], iface_ref[...]).astype(BF)
    push(if_send.at[1], if_recv.at[1], 19, 0, 0, (prv, f))

    @pl.when(f != z)
    def _():
        await_slot(xr_recv, 14, 0)

    x_own = dot_t(xr_recv[...], place)
    mx_own = (x_own * mroot_ref[...]).astype(BF)

    mass_x = xs_acc[...] * mass_ref[...]
    await_slot(if_recv.at[0], 18, 0)
    first = mass_x[:, :RIM] + dot_t(if_recv[0], iface_ref[...])
    await_slot(if_recv.at[1], 19, 0)
    last = mass_x[:, SH - RIM :] + if_recv[1].astype(F32)
    mx = jnp.concatenate([first, last], axis=1).astype(BF)

    load_bas.wait()
    load_brt.wait()
    brt[pl.ds(RR, PAD - RR), :] = jnp.zeros((PAD - RR, NB), BF)
    for k in range(1, NF + 1):
        p = lax.rem(f + k, NF)
        cols = pl.ds(pl.multiple_of(p * NBS, 128), NBS)
        piece = (dot(mx, bas[:, cols]) + dot(mx_own, brt[:, cols])).astype(BF)
        if k < NF:
            g_send[k] = piece
            push(g_send.at[k], g_recv.at[f], 20, k, f, dev_f(p))
        else:
            g_recv[f] = piece
    await_ring(g_recv, 20, f, NF)
    part = sum(g_recv[j].astype(F32) for j in range(NF)).astype(BF)
    g_ysend[...] = part.reshape(NY, N // NY, NBS)
    g_yrecv[y] = g_ysend[y]
    for k in range(1, NY):
        p = lax.rem(y + k, NY)
        push(g_ysend.at[p], g_yrecv.at[y], 21, k, y, dev_y(p))
    await_ring(g_yrecv, 21, y, NY)
    g_zall[z] = sum(g_yrecv[j].astype(F32) for j in range(NY)).astype(BF)
    for k in range(1, NZ):
        push(g_zall.at[z], g_zall.at[z], 22, k, z, dev_z(lax.rem(z + k, NZ)))
    await_ring(g_zall, 22, z, NZ)
    g_yall[y] = sum(g_zall[j].astype(F32) for j in range(NZ)).astype(BF)
    for k in range(1, NY):
        push(g_yall.at[y], g_yall.at[y], 23, k, y, dev_y(lax.rem(y + k, NY)))
    await_ring(g_yall, 23, y, NY)
    g_all[f] = g_yall[...].reshape(N, NBS)
    for k in range(1, NF):
        push(g_all.at[f], g_all.at[f], 24, k, f, dev_f(lax.rem(f + k, NF)))
    new_sub_ref[...] = xs_acc[...]
    new_root_ref[...] = x_own
    for k in range(NF):
        p = lax.rem(f + NF - k, NF)
        if k:
            await_slot(g_all.at[p], 24, p)
        cols = pl.ds(pl.multiple_of(p * NBS, 128), NBS)
        gram_ref[:, cols] = g_all[p].astype(F32)
        new_sub_ref[...] -= dot_t(g_all[p], bas[:, cols])
        new_root_ref[...] -= dot_t(g_all[p], brt[:, cols])

    for copy, cond in sends:
        if cond is None:
            copy.wait_send()
        else:
            pl.when(cond)(copy.wait_send)


def body(
    rhs_sub,
    rhs_root,
    factor_sub,
    coupling,
    update_rows,
    factor_root,
    mass_sub,
    mass_root,
    interface,
    basis_sub,
    basis_root,
):
    rhs_t = rhs_sub.astype(BF).T
    root_t = jnp.pad(rhs_root.astype(BF).T, ((0, 0), (0, PAD - RR)))
    mroot = jnp.pad(mass_root, (0, PAD - RR))[None, :]
    vmem = pl.BlockSpec(memory_space=pltpu.VMEM)
    hbm = pl.BlockSpec(memory_space=pl.ANY)
    leaf_sum = [
        pltpu.VMEM((NY, N, GR), BF),
        pltpu.VMEM((NY, N, GR), BF),
        pltpu.VMEM((NZ, N // NZ, GR), F32),
        pltpu.VMEM((NZ, N // NZ, GR), F32),
        pltpu.VMEM((NZ, N // NZ, GR), F32),
        pltpu.VMEM((NY, N, GR), BF),
    ]
    new_sub, new_root, gram = pl.pallas_call(
        kernel,
        out_shape=(
            jax.ShapeDtypeStruct((N, SH), F32),
            jax.ShapeDtypeStruct((N, PAD), F32),
            jax.ShapeDtypeStruct((N, NB), F32),
        ),
        in_specs=[vmem, vmem, hbm, hbm, vmem, hbm, vmem, vmem, vmem, hbm, hbm],
        out_specs=(vmem, vmem, vmem),
        scratch_shapes=[
            pltpu.VMEM((SH, SUB), BF),
            pltpu.VMEM((UP, SH), BF),
            pltpu.VMEM((SL, UP), BF),
            pltpu.VMEM((GR, SL), BF),
            pltpu.VMEM((SH, NB), BF),
            pltpu.VMEM((PAD, NB), BF),
            pltpu.VMEM((NF, N, SH), BF),
            pltpu.VMEM((N, GR), BF),
            pltpu.VMEM((NF, N, GR), BF),
            pltpu.VMEM((N, GR), F32),
            pltpu.VMEM((N, SH), F32),
            pltpu.VMEM((NF, N, UPS), BF),
            pltpu.VMEM((NF, N, UPS), BF),
            pltpu.VMEM((NF, N, UPS), BF),
            *leaf_sum,
            pltpu.VMEM((NF, N, GR), BF),
            *leaf_sum,
            pltpu.VMEM((N, GR), BF),
            pltpu.VMEM((NF, N, UPS), BF),
            pltpu.VMEM((NF, N, UPS), BF),
            pltpu.VMEM((NF, N, UPS), BF),
            pltpu.VMEM((NF, N, SH), BF),
            pltpu.VMEM((NF, N, SH), BF),
            pltpu.VMEM((N, SH), F32),
            pltpu.VMEM((2, N, RIM), BF),
            pltpu.VMEM((2, N, RIM), BF),
            pltpu.VMEM((NF, N, NBS), BF),
            pltpu.VMEM((NF, N, NBS), BF),
            pltpu.VMEM((NY, N // NY, NBS), BF),
            pltpu.VMEM((NY, N // NY, NBS), BF),
            pltpu.VMEM((NZ, N // NY, NBS), BF),
            pltpu.VMEM((NY, N // NY, NBS), BF),
            pltpu.VMEM((NF, N, NBS), BF),
            pltpu.SemaphoreType.DMA((STAGES, 8)),
            pltpu.SemaphoreType.DMA((STAGES, 8)),
            pltpu.SemaphoreType.DMA((8,)),
        ],
        compiler_params=pltpu.CompilerParams(
            collective_id=0, has_side_effects=True, vmem_limit_bytes=48 * 1024 * 1024
        ),
    )(
        rhs_t,
        root_t,
        factor_sub[0],
        coupling[0],
        update_rows,
        factor_root,
        mass_sub[None, :],
        mroot,
        interface[0],
        basis_sub,
        basis_root,
    )
    return new_sub.T, new_root[:, :RR].T, gram.T


def solution(mesh):
    placed = (
        P(("leaf", "front"), None),
        P(("leaf", "front"), None),
        P("leaf", "front", None),
        P("leaf", None, "front"),
        P("leaf", None),
        P(("leaf", "front"), None),
        P(("leaf", "front")),
        P(("leaf", "front")),
        P(("leaf", "front"), None, None),
        P(("leaf", "front"), None),
        P(("leaf", "front"), None),
    )
    return jax.shard_map(
        body,
        mesh=mesh,
        in_specs=placed,
        out_specs=(P(("leaf", "front"), None), P(("leaf", "front"), None), P()),
        check_vma=False,
    )
```

```python
import jax
import jax.numpy as jnp
from jax import lax
from jax.experimental import pallas as pl
from jax.experimental.pallas import tpu as pltpu
from jax.sharding import PartitionSpec as P

BF = jnp.bfloat16
F32 = jnp.float32
MESH = pl.DeviceIdType.MESH

N = 64
NF = 8
NY = 4
NZ = 8
NX = 4
NC = 2
NG = NY * NZ
NS = 4
NR = NY * NS
SH = 512
SUB = NF * SH
UP = 2048
UPS = UP // NF
RR = 48
GR = NF * RR
SL = NY * GR
ROOT = NF * SL
RIM = 256
NB = 2048
NBS = NB // NF
PAD = 128
SENDS = 240
RECVS = 160


def dot(a, b):
    return jnp.dot(a, b, preferred_element_type=F32)


def dot_t(a, b):
    return lax.dot_general(a, b, (((1,), (1,)), ((), ())), preferred_element_type=F32)


def kernel(
    rhs_hbm,
    rroot_hbm,
    factor_hbm,
    coupling_hbm,
    rows_hbm,
    froot_hbm,
    mass_hbm,
    mroot_hbm,
    iface_hbm,
    basis_hbm,
    broot_hbm,
    new_sub_ref,
    new_root_ref,
    gram_ref,
    rhs_in,
    rroot_in,
    fac,
    cpl,
    rows_ref,
    frs,
    mass_ref,
    mroot_in,
    iface_ref,
    bas,
    brt,
    onehot,
    frt,
    rhs_all,
    rr_send,
    rr_all,
    rr_sum,
    y_acc,
    up_send,
    up_recv,
    up_all,
    d_send,
    d_recv,
    d_all,
    yr_send,
    yr_sib,
    yr_all,
    x_send,
    x_recv,
    x_all,
    xr_recv,
    pk_send,
    pk_recv,
    pk_all,
    xb_send,
    xb_recv,
    xs_send,
    xs_recv,
    xs_acc,
    if_send,
    if_recv,
    gc_send,
    gc_recv,
    gc_own,
    gp_send,
    gp_recv,
    gz_all,
    g_all,
    ssem,
    rsem,
    lsem,
):
    g = lax.axis_index("leaf")
    f = lax.axis_index("front")
    z = lax.div(g, NY)
    y = lax.rem(g, NY)
    x = lax.div(f, NC)
    c = lax.rem(f, NC)
    other = 1 - c

    def dev_f(i):
        return (g, i)

    def dev_x(i):
        return (g, i * NC + c)

    def dev_z(i):
        return (i * NY + y, f)

    def dev_xy(i, j):
        return (z * NY + j, i * NC + c)

    def turn(a, k, n):
        return lax.rem(a + k, n)

    loads = [
        (rhs_hbm, rhs_in),
        (rroot_hbm, rroot_in),
        (rows_hbm, rows_ref),
        (factor_hbm, fac),
        (froot_hbm, frs),
        (coupling_hbm, cpl),
        (iface_hbm, iface_ref),
        (mass_hbm, mass_ref),
        (mroot_hbm, mroot_in),
        (broot_hbm, brt),
        (basis_hbm, bas),
    ]
    loads = [pltpu.make_async_copy(a, b, lsem.at[i]) for i, (a, b) in enumerate(loads)]
    (
        load_rhs,
        load_rroot,
        load_rows,
        load_fac,
        load_frs,
        load_cpl,
        load_iface,
        load_mass,
        load_mroot,
        load_brt,
        load_bas,
    ) = loads
    for load in loads:
        load.start()

    barrier = pltpu.get_barrier_semaphore()
    peers = [dev_f(turn(f, k, NF)) for k in range(1, NF)]
    peers += [(turn(g, k, NG), f) for k in range(1, NG)]
    peers += [
        dev_xy(turn(x, i, NX), turn(y, j, NY)) for i in range(1, NX) for j in range(1, NY)
    ]
    for dev in peers:
        pl.semaphore_signal(barrier, inc=1, device_id=dev, device_id_type=MESH)

    sends = []
    slots = [0]

    def take(n):
        slots[0] += n
        assert slots[0] <= RECVS
        return slots[0] - n

    def push(src, dst, slot, dev, cond=None):
        assert len(sends) < SENDS
        copy = pltpu.make_async_remote_copy(
            src_ref=src,
            dst_ref=dst,
            send_sem=ssem.at[len(sends)],
            recv_sem=rsem.at[slot],
            device_id=dev,
            device_id_type=MESH,
        )
        if cond is None:
            copy.start()
        else:
            pl.when(cond)(copy.start)
        sends.append((copy, cond))

    def land(buf, slot):
        pltpu.make_async_remote_copy(
            src_ref=buf,
            dst_ref=buf,
            send_sem=ssem.at[0],
            recv_sem=rsem.at[slot],
            device_id=(g, f),
            device_id_type=MESH,
        ).wait_recv()

    def land_ring(buf, base, me, n):
        for k in range(1, n):
            p = turn(me, n - k, n)
            land(buf.at[p], base + p)

    spot = lax.broadcasted_iota(jnp.int32, (PAD, GR), 0)
    lane = lax.broadcasted_iota(jnp.int32, (PAD, GR), 1)
    place = jnp.where((lane == spot + f * RR) & (spot < RR), 1.0, 0.0).astype(BF)
    unit = jnp.where(
        lax.broadcasted_iota(jnp.int32, (N, N), 0) == lax.broadcasted_iota(jnp.int32, (N, N), 1),
        1.0,
        0.0,
    ).astype(BF)
    load_rhs.wait()
    rhs_all[f] = rhs_in[...].astype(BF)
    load_rroot.wait()
    rr_mine = dot(dot_t(unit, rroot_in[...].astype(BF)).astype(BF), place[:RR]).astype(BF)
    rr_send[...] = rr_mine
    rr_all[f] = rr_mine

    pl.semaphore_wait(barrier, len(peers))

    at = take(NF)
    for k in range(1, NF):
        push(rhs_all.at[f], rhs_all.at[f], at + f, dev_f(turn(f, k, NF)), f + k < NF)
    at_rhs = at
    at_rr = take(NF)
    push(rr_send, rr_all.at[f], at_rr + f, dev_f(z), f != z)

    load_rows.wait()

    def hot(i, _):
        rows = pl.ds(pl.multiple_of(i * 64, 64), 64)
        ids = lax.broadcasted_iota(jnp.int32, (64, UP), 0) + (f * SL + i * 64)
        onehot[rows, :] = jnp.where(ids == rows_ref[...], 1.0, 0.0).astype(BF)
        return 0

    lax.fori_loop(0, SL // 64, hot, 0)

    load_fac.wait()
    mine = pl.ds(pl.multiple_of(f * SH, 128), SH)
    below = lax.broadcasted_iota(jnp.int32, (SH, SH), 1) <= lax.broadcasted_iota(
        jnp.int32, (SH, SH), 0
    )
    diag = jnp.where(below, fac[:, mine].astype(F32), 0.0).astype(BF)
    fac[:, mine] = diag
    y_acc[...] = dot_t(rhs_all[f], diag)

    load_frs.wait()

    def lower(j, _):
        cols = pl.ds(pl.multiple_of(j * SL, 128), SL)
        row_ids = lax.broadcasted_iota(jnp.int32, (RR, SL), 0) + (g * GR + f * RR)
        col_ids = lax.broadcasted_iota(jnp.int32, (RR, SL), 1) + j * SL
        frs[:, cols] = jnp.where(col_ids <= row_ids, frs[:, cols].astype(F32), 0.0).astype(BF)
        return 0

    lax.fori_loop(0, NF, lower, 0)
    for k in range(1, NF):

        @pl.when(f >= k)
        def _(k=k):
            p = f - k
            land(rhs_all.at[p], at_rhs + p)
            cols = pl.ds(pl.multiple_of(p * SH, 128), SH)
            y_acc[...] += dot_t(rhs_all[p], fac[:, cols])

    y_low = y_acc[...].astype(BF)

    load_cpl.wait()
    at = take(NF)
    for k in range(1, NF + 1):
        p = turn(f, k, NF)
        rows = pl.ds(pl.multiple_of(p * UPS, 128), UPS)
        piece = dot_t(y_low, cpl[rows, :]).astype(BF)
        if k < NF:
            up_send[k] = piece
            push(up_send.at[k], up_recv.at[f], at + f, dev_f(p))
        else:
            up_recv[f] = piece
    land_ring(up_recv, at, f, NF)
    up_all[f] = sum(up_recv[j].astype(F32) for j in range(NF)).astype(BF)
    at = take(NF)
    for k in range(1, NF):
        push(up_all.at[f], up_all.at[f], at + f, dev_f(turn(f, k, NF)))

    at_frt = take(NF)
    my_rows = pl.ds(pl.multiple_of(f * RR, 16), RR)
    for k in range(1, NF):
        p = turn(f, k, NF)
        cols = pl.ds(pl.multiple_of(p * SL, 128), SL)
        push(frs.at[:, cols], frt.at[my_rows], at_frt + f, dev_f(p))
    frt[my_rows, :] = frs[:, pl.ds(pl.multiple_of(f * SL, 128), SL)]

    @pl.when(f == z)
    def _():
        land_ring(rr_all, at_rr, f, NF)
        rr_sum[...] = sum(rr_all[j].astype(F32) for j in range(NF))

    @pl.when(f != z)
    def _():
        rr_sum[...] = jnp.zeros_like(rr_sum)

    land_ring(up_all, at, f, NF)

    adds = lax.rem(z + y + c, 2) == 0
    spot_mine = 2 * z + lax.div(y, 2)

    def leaf_sum(chunk, send, recv, full):
        at_sum = take(1)
        at_full = take(1)
        for turn_q in (2, 1, 3, 0):
            q = turn(lax.div(z, 2), turn_q, NY)
            send[q] = chunk(q).astype(BF).reshape(NS, N // NS, GR)
            for s in range(NS):
                zi = 2 * q + s // 2
                to = zi * NY + 2 * (s % 2) + lax.rem(zi + c, 2)
                slot = lax.rem(g - to + NG - 1, NG)
                push(send.at[q, s], recv.at[slot], at_sum, (to, f), to != g)

        @pl.when(adds)
        def _():
            land(recv.at[pl.ds(0, NG - 1)], at_sum)
            q = lax.div(spot_mine, NS)
            total = send[q, lax.rem(spot_mine, NS)].astype(F32)
            for j in range(NG - 1):
                total += recv[j].astype(F32)
            full[spot_mine] = total.astype(BF)

        for k in sorted(range(1, NG), key=lambda k: -min(k, NG - k)):
            to = turn(g, k, NG)
            push(full.at[spot_mine], full.at[spot_mine], at_full, (to, f), adds)

        @pl.when(adds)
        def _():
            land(full.at[pl.ds(0, NR - 1)], at_full)

        @pl.when(jnp.logical_not(adds))
        def _():
            land(full, at_full)

        parts = [full[pl.ds(NS * j, NS)].reshape(N, GR) for j in range(NY)]
        return jnp.concatenate(parts, axis=1)

    up_low = jnp.concatenate([up_all[j] for j in range(NF)], axis=1)

    def scatter_chunk(q):
        total = dot_t(up_low, onehot[pl.ds(pl.multiple_of(q * GR, 128), GR), :])
        return jnp.where(q == y, rr_sum[...], 0.0) - total

    b_low = leaf_sum(scatter_chunk, d_send, d_recv, d_all)

    land_ring_rows = [turn(f, NF - k, NF) for k in range(1, NF)]
    for p in land_ring_rows:
        land(frt.at[pl.ds(pl.multiple_of(p * RR, 16), RR)], at_frt + p)
    yr_send[...] = dot_t(b_low, frt[...]).astype(BF)
    at = take(1)
    push(yr_send, yr_sib, at, dev_f(x * NC + other))
    land(yr_sib, at)
    yr_all[x] = (yr_send[...].astype(F32) + yr_sib[...].astype(F32)).astype(BF)
    at = take(NX)
    for k in (2, 1, 3):
        push(yr_all.at[x], yr_all.at[x], at + x, dev_x(turn(x, k, NX)))
    land_ring(yr_all, at, x, NX)
    yr_low = sum(yr_all[j].astype(F32) for j in range(NX)).astype(BF)

    def back_chunk(q):
        return dot(yr_low, frt[:, pl.ds(pl.multiple_of(q * GR, 128), GR)])

    x_low = leaf_sum(back_chunk, x_send, x_recv, x_all)

    at = take(NF)
    for k in range(1, NF + 1):
        p = turn(f, k, NF)
        cols = pl.ds(pl.multiple_of(p * UPS, 128), UPS)
        piece = dot(x_low, onehot[:, cols]).astype(BF)
        if k < NF:
            pk_send[k] = piece
            push(pk_send.at[k], pk_recv.at[f], at + f, dev_f(p))
        else:
            pk_recv[f] = piece
    land_ring(pk_recv, at, f, NF)
    pk_all[f] = sum(pk_recv[j].astype(F32) for j in range(NF)).astype(BF)
    at = take(NF)
    for k in range(1, NF):
        push(pk_all.at[f], pk_all.at[f], at + f, dev_f(turn(f, k, NF)))
    at_xr = take(1)
    block = pl.ds(pl.multiple_of(NS * y, NS), NS)
    for k in range(1, NF):
        push(x_all.at[block], xr_recv, at_xr, dev_f(turn(f, k, NF)), f == z)

    @pl.when(f == z)
    def _():
        xr_recv[...] = x_all[block]

    for k in range(NF):
        p = turn(f, NF - k, NF)
        if k:
            land(pk_all.at[p], at + p)
        rows = pl.ds(pl.multiple_of(p * UPS, 128), UPS)
        y_acc[...] -= dot(pk_all[p], cpl[rows, :])
    t_low = y_acc[...].astype(BF)

    at = take(NX)
    for k in range(NX):
        used = (x >= k) if k else (c == 1)
        i = turn(x, NX - k, NX)

        @pl.when(used)
        def _(i=i):
            cols = pl.ds(pl.multiple_of((i * NC + other) * SH, 128), SH)
            xb_send[i] = dot(t_low, fac[:, cols]).astype(BF)

        push(xb_send.at[i], xb_recv.at[i], at + i, dev_f(x * NC + other), used)
    at_xs = take(NX)
    for k in (1, 2, 3, 0):
        used = x >= k
        i = turn(x, NX - k, NX)
        cols = pl.ds(pl.multiple_of((i * NC + c) * SH, 128), SH)
        if k:

            @pl.when(used)
            def _(i=i, cols=cols):
                part = dot(t_low, fac[:, cols])
                land(xb_recv.at[i], at + i)
                xs_send[i] = (part + xb_recv[i].astype(F32)).astype(BF)

            push(xs_send.at[i], xs_recv.at[x], at_xs + x, dev_x(i), used)
        else:
            xs_acc[...] = dot(t_low, fac[:, cols])

            @pl.when(c == 0)
            def _(i=i):
                land(xb_recv.at[i], at + i)
                xs_acc[...] += xb_recv[i].astype(F32)

    for k in range(1, NX):

        @pl.when(x + k < NX)
        def _(k=k):
            land(xs_recv.at[x + k], at_xs + x + k)
            xs_acc[...] += xs_recv[x + k].astype(F32)

    at_next = take(1)
    at_prev = take(1)
    xs_low = xs_acc[...].astype(BF)
    if_send[0] = xs_low[:, SH - RIM :]
    push(if_send.at[0], if_recv.at[0], at_next, (turn(g, 1, NG), f))
    load_iface.wait()
    if_send[1] = dot(xs_low[:, :RIM], iface_ref[...]).astype(BF)
    push(if_send.at[1], if_recv.at[1], at_prev, (turn(g, NG - 1, NG), f))

    @pl.when(f != z)
    def _():
        land(xr_recv, at_xr)

    load_mroot.wait()
    x_own = dot_t(xr_recv[...].reshape(N, GR), place)
    new_root_ref[...] = dot_t(place, xr_recv[...].reshape(N, GR))[:RR]
    mx_own = (x_own[:, :RR] * mroot_in[...]).astype(BF)
    load_brt.wait()

    load_mass.wait()
    mass_x = xs_acc[...] * mass_ref[...]
    new_sub_ref[...] = xs_acc[...]
    land(if_recv.at[0], at_next)
    first = mass_x[:, :RIM] + dot_t(if_recv[0], iface_ref[...])
    land(if_recv.at[1], at_prev)
    last = mass_x[:, SH - RIM :] + if_recv[1].astype(F32)
    mx = jnp.concatenate([first, last], axis=1).astype(BF)

    load_bas.wait()

    def gram_part(block):
        cols = pl.ds(pl.multiple_of(block * NBS, 128), NBS)
        return dot(mx, bas[:, cols]) + dot(mx_own, brt[:, cols])

    at = take(NX)
    for j in range(NX):
        gc_send[j] = gram_part(other * NX + j).astype(BF)
        push(gc_send.at[j], gc_recv.at[j], at + j, dev_f(x * NC + other))
    for j in range(NX):
        gc_own[j] = gram_part(c * NX + j)
    at_p = take(1)
    for i in (2, 1, 3, 0):
        xi = turn(x, i, NX)
        land(gc_recv.at[xi], at + xi)
        part = gc_own[xi] + gc_recv[xi].astype(F32)
        gp_send[xi] = part.astype(BF).reshape(NY, N // NY, NBS)
        for j in (2, 1, 3, 0):
            if i or j:
                yj = turn(y, j, NY)
                slot = ((NX - i) % NX) * NY + (NY - j) % NY - 1
                push(gp_send.at[xi, yj], gp_recv.at[slot], at_p, dev_xy(xi, yj))
    land(gp_recv, at_p)
    total = gp_send[x, y].astype(F32)
    for j in range(NX * NY - 1):
        total += gp_recv[j].astype(F32)
    gz_all[z] = total.astype(BF)
    at = take(NZ)
    for k in (4, 3, 5, 2, 6, 1, 7):
        push(gz_all.at[z], gz_all.at[z], at + z, dev_z(turn(z, k, NZ)))
    land_ring(gz_all, at, z, NZ)
    mine = c * NX + x
    g_all[mine, y] = sum(gz_all[j].astype(F32) for j in range(NZ)).astype(BF)
    at = take(1)
    for i in (2, 1, 3, 0):
        for j in (2, 1, 3, 0):
            if i or j:
                to = dev_xy(turn(x, i, NX), turn(y, j, NY))
                push(g_all.at[mine, y], g_all.at[mine, y], at, to)
    land(gp_recv, at)
    at = take(1)
    half = pl.ds(pl.multiple_of(c * NX, NX), NX)
    push(g_all.at[half], g_all.at[half], at, dev_f(x * NC + other))

    def apply(block):
        cols = pl.ds(pl.multiple_of(block * NBS, 128), NBS)
        low = g_all[block].reshape(N, NBS)
        gram_ref[:, cols] = low.astype(F32)
        new_sub_ref[...] -= dot_t(low, bas[:, cols])
        new_root_ref[...] -= dot_t(brt[:, cols], low)

    for j in range(NX):
        apply(c * NX + j)
    land(g_all.at[pl.ds(pl.multiple_of(other * NX, NX), NX)], at)
    for j in range(NX):
        apply(other * NX + j)

    for copy, cond in sends:
        if cond is None:
            copy.wait_send()
        else:
            pl.when(cond)(copy.wait_send)


def body(
    rhs_sub,
    rhs_root,
    factor_sub,
    coupling,
    update_rows,
    factor_root,
    mass_sub,
    mass_root,
    interface,
    basis_sub,
    basis_root,
):
    vmem = pl.BlockSpec(memory_space=pltpu.VMEM)
    hbm = pl.BlockSpec(memory_space=pl.ANY)
    leaf_sum = [
        pltpu.VMEM((NY, NS, N // NS, GR), BF),
        pltpu.VMEM((NG, N // NS, GR), BF),
        pltpu.VMEM((NR, N // NS, GR), BF),
    ]
    new_sub, new_root, gram = pl.pallas_call(
        kernel,
        out_shape=(
            jax.ShapeDtypeStruct((N, SH), F32),
            jax.ShapeDtypeStruct((RR, N), F32),
            jax.ShapeDtypeStruct((N, NB), F32),
        ),
        in_specs=[hbm] * 11,
        out_specs=(vmem, vmem, vmem),
        scratch_shapes=[
            pltpu.VMEM((N, SH), F32),
            pltpu.VMEM((RR, N), F32),
            pltpu.VMEM((SH, SUB), BF),
            pltpu.VMEM((UP, SH), BF),
            pltpu.VMEM((1, UP), jnp.int32),
            pltpu.VMEM((RR, ROOT), BF),
            pltpu.VMEM((1, SH), F32),
            pltpu.VMEM((1, RR), F32),
            pltpu.VMEM((RIM, RIM), BF),
            pltpu.VMEM((SH, NB), BF),
            pltpu.VMEM((RR, NB), BF),
            pltpu.VMEM((SL, UP), BF),
            pltpu.VMEM((GR, SL), BF),
            pltpu.VMEM((NF, N, SH), BF),
            pltpu.VMEM((N, GR), BF),
            pltpu.VMEM((NF, N, GR), BF),
            pltpu.VMEM((N, GR), F32),
            pltpu.VMEM((N, SH), F32),
            pltpu.VMEM((NF, N, UPS), BF),
            pltpu.VMEM((NF, N, UPS), BF),
            pltpu.VMEM((NF, N, UPS), BF),
            *leaf_sum,
            pltpu.VMEM((N, GR), BF),
            pltpu.VMEM((N, GR), BF),
            pltpu.VMEM((NX, N, GR), BF),
            *leaf_sum,
            pltpu.VMEM((NS, N // NS, GR), BF),
            pltpu.VMEM((NF, N, UPS), BF),
            pltpu.VMEM((NF, N, UPS), BF),
            pltpu.VMEM((NF, N, UPS), BF),
            pltpu.VMEM((NX, N, SH), BF),
            pltpu.VMEM((NX, N, SH), BF),
            pltpu.VMEM((NX, N, SH), BF),
            pltpu.VMEM((NX, N, SH), BF),
            pltpu.VMEM((N, SH), F32),
            pltpu.VMEM((2, N, RIM), BF),
            pltpu.VMEM((2, N, RIM), BF),
            pltpu.VMEM((NX, N, NBS), BF),
            pltpu.VMEM((NX, N, NBS), BF),
            pltpu.VMEM((NX, N, NBS), F32),
            pltpu.VMEM((NX, NY, N // NY, NBS), BF),
            pltpu.VMEM((NX * NY - 1, N // NY, NBS), BF),
            pltpu.VMEM((NZ, N // NY, NBS), BF),
            pltpu.VMEM((NF, NY, N // NY, NBS), BF),
            pltpu.SemaphoreType.DMA((SENDS,)),
            pltpu.SemaphoreType.DMA((RECVS,)),
            pltpu.SemaphoreType.DMA((16,)),
        ],
        compiler_params=pltpu.CompilerParams(
            collective_id=0, has_side_effects=True, vmem_limit_bytes=56 * 1024 * 1024
        ),
    )(
        rhs_sub.T,
        rhs_root,
        factor_sub[0],
        coupling[0],
        update_rows,
        factor_root,
        mass_sub[None, :],
        mass_root[None, :],
        interface[0],
        basis_sub,
        basis_root,
    )
    return new_sub.T, new_root, gram.T


def solution(mesh):
    placed = (
        P(("leaf", "front"), None),
        P(("leaf", "front"), None),
        P("leaf", "front", None),
        P("leaf", None, "front"),
        P("leaf", None),
        P(("leaf", "front"), None),
        P(("leaf", "front")),
        P(("leaf", "front")),
        P(("leaf", "front"), None, None),
        P(("leaf", "front"), None),
        P(("leaf", "front"), None),
    )
    return jax.shard_map(
        body,
        mesh=mesh,
        in_specs=placed,
        out_specs=(P(("leaf", "front"), None), P(("leaf", "front"), None), P()),
        check_vma=False,
    )
```

```python
import jax
import jax.numpy as jnp
from jax import lax
from jax.experimental import pallas as pl
from jax.experimental.pallas import tpu as pltpu
from jax.sharding import PartitionSpec as P

BF = jnp.bfloat16
F32 = jnp.float32
MESH = pl.DeviceIdType.MESH

N = 64
NF = 8
NY = 4
NZ = 8
NX = 4
NC = 2
NG = NY * NZ
NS = 4
NR = NY * NS
SH = 512
SUB = NF * SH
UP = 2048
UPS = UP // NF
RR = 48
GR = NF * RR
SL = NY * GR
ROOT = NF * SL
RIM = 256
NB = 2048
NBS = NB // NF
PAD = 128
STEP = 4
ORDER = (4, 5, 3, 2, 6, 7, 1)
SENDS = 240
RECVS = 160


def dot(a, b):
    return jnp.dot(a, b, preferred_element_type=F32)


def dot_t(a, b):
    return lax.dot_general(a, b, (((1,), (1,)), ((), ())), preferred_element_type=F32)


def kernel(
    rhs_hbm,
    rroot_hbm,
    factor_hbm,
    coupling_hbm,
    rows_hbm,
    froot_hbm,
    mass_hbm,
    mroot_hbm,
    iface_hbm,
    basis_hbm,
    broot_hbm,
    xs_hbm,
    xr_hbm,
    g_hbm,
    rhs_in,
    rroot_in,
    fac,
    cpl,
    rows_ref,
    frs,
    mass_ref,
    mroot_in,
    iface_ref,
    bas,
    brt,
    onehot,
    frt,
    rhs_all,
    rr_send,
    rr_all,
    rr_sum,
    y_acc,
    up_send,
    up_recv,
    up_all,
    d_send,
    d_recv,
    d_all,
    yr_send,
    yr_sib,
    yr_all,
    x_send,
    x_recv,
    x_all,
    xr_send,
    xr_recv,
    pk_send,
    pk_recv,
    pk_all,
    xb_send,
    xb_recv,
    xs_send,
    xs_recv,
    xs_acc,
    xr_out,
    if_send,
    if_recv,
    gc_send,
    gc_recv,
    gc_own,
    gp_send,
    gp_recv,
    gz_all,
    g_all,
    ssem,
    rsem,
    lsem,
):
    g = lax.axis_index("leaf")
    f = lax.axis_index("front")
    z = lax.div(g, NY)
    y = lax.rem(g, NY)
    x = lax.div(f, NC)
    c = lax.rem(f, NC)
    other = 1 - c

    def dev_f(i):
        return (g, i)

    def dev_x(i):
        return (g, i * NC + c)

    def dev_z(i):
        return (i * NY + y, f)

    def dev_xy(i, j):
        return (z * NY + j, i * NC + c)

    def turn(a, k, n):
        return lax.rem(a + k, n)

    loads = [
        (rhs_hbm, rhs_in),
        (rroot_hbm, rroot_in),
        (rows_hbm, rows_ref),
        (factor_hbm, fac),
        (froot_hbm, frs),
        (coupling_hbm, cpl),
        (iface_hbm, iface_ref),
        (mass_hbm, mass_ref),
        (mroot_hbm, mroot_in),
        (broot_hbm, brt),
        (basis_hbm, bas),
    ]
    loads = [pltpu.make_async_copy(a, b, lsem.at[i]) for i, (a, b) in enumerate(loads)]
    (
        load_rhs,
        load_rroot,
        load_rows,
        load_fac,
        load_frs,
        load_cpl,
        load_iface,
        load_mass,
        load_mroot,
        load_brt,
        load_bas,
    ) = loads
    for load in loads:
        load.start()

    barrier = pltpu.get_barrier_semaphore()
    def hops(k, n):
        return min(k, n - k)

    peers = [(hops(i, NX), (g, turn(x, i, NX) * NC + c)) for i in range(1, NX)]
    peers += [(hops(i, NX), (g, turn(x, i, NX) * NC + other)) for i in range(NX)]
    peers += [
        (hops(j, NY) + hops(i, NZ), (turn(z, i, NZ) * NY + turn(y, j, NY), f))
        for i in range(NZ)
        for j in range(NY)
        if i or j
    ]
    peers += [
        (hops(i, NX) + hops(j, NY), dev_xy(turn(x, i, NX), turn(y, j, NY)))
        for i in range(1, NX)
        for j in range(1, NY)
    ]
    for _, dev in sorted(peers, key=lambda peer: -peer[0]):
        pl.semaphore_signal(barrier, inc=1, device_id=dev, device_id_type=MESH)

    sends = []
    slots = [0]

    def take(n):
        slots[0] += n
        assert slots[0] <= RECVS
        return slots[0] - n

    def push(src, dst, slot, dev, cond=None):
        assert len(sends) < SENDS
        copy = pltpu.make_async_remote_copy(
            src_ref=src,
            dst_ref=dst,
            send_sem=ssem.at[len(sends)],
            recv_sem=rsem.at[slot],
            device_id=dev,
            device_id_type=MESH,
        )
        if cond is None:
            copy.start()
        else:
            pl.when(cond)(copy.start)
        sends.append((copy, cond))

    def land(buf, slot):
        pltpu.make_async_remote_copy(
            src_ref=buf,
            dst_ref=buf,
            send_sem=ssem.at[0],
            recv_sem=rsem.at[slot],
            device_id=(g, f),
            device_id_type=MESH,
        ).wait_recv()

    def land_ring(buf, base, me, n):
        for k in range(1, n):
            p = turn(me, n - k, n)
            land(buf.at[p], base + p)

    spot = lax.broadcasted_iota(jnp.int32, (PAD, GR), 0)
    lane = lax.broadcasted_iota(jnp.int32, (PAD, GR), 1)

    def place(j):
        return jnp.where((lane == spot + j * RR) & (spot < RR), 1.0, 0.0).astype(BF)

    widen = jnp.where(
        lax.broadcasted_iota(jnp.int32, (RR, PAD), 0)
        == lax.broadcasted_iota(jnp.int32, (RR, PAD), 1),
        1.0,
        0.0,
    ).astype(BF)
    unit = jnp.where(
        lax.broadcasted_iota(jnp.int32, (N, N), 0) == lax.broadcasted_iota(jnp.int32, (N, N), 1),
        1.0,
        0.0,
    ).astype(BF)
    load_rhs.wait()
    rhs_all[f] = rhs_in[...].astype(BF)
    load_rroot.wait()
    rr_mine = dot(dot_t(unit, rroot_in[...].astype(BF)).astype(BF), widen).astype(BF)
    rr_send[...] = rr_mine
    rr_all[f] = rr_mine

    pl.semaphore_wait(barrier, len(peers))

    at = take(NF)
    for k in range(1, NF):
        push(rhs_all.at[f], rhs_all.at[f], at + f, dev_f(turn(f, k, NF)), f + k < NF)
    at_rhs = at
    at_rr = take(NF)
    push(rr_send, rr_all.at[f], at_rr + f, dev_f(z), f != z)

    load_rows.wait()

    def hot(i, _):
        rows = pl.ds(pl.multiple_of(i * 64, 64), 64)
        ids = lax.broadcasted_iota(jnp.int32, (64, UP), 0) + (f * SL + i * 64)
        onehot[rows, :] = jnp.where(ids == rows_ref[...], 1.0, 0.0).astype(BF)
        return 0

    lax.fori_loop(0, SL // 64, hot, 0)

    load_fac.wait()
    mine = pl.ds(pl.multiple_of(f * SH, 128), SH)
    below = lax.broadcasted_iota(jnp.int32, (SH, SH), 1) <= lax.broadcasted_iota(
        jnp.int32, (SH, SH), 0
    )
    diag = jnp.where(below, fac[:, mine].astype(F32), 0.0).astype(BF)
    fac[:, mine] = diag
    y_acc[...] = dot_t(rhs_all[f], diag)

    load_frs.wait()

    def lower(j, _):
        cols = pl.ds(pl.multiple_of(j * SL, 128), SL)
        row_ids = lax.broadcasted_iota(jnp.int32, (RR, SL), 0) + (g * GR + f * RR)
        col_ids = lax.broadcasted_iota(jnp.int32, (RR, SL), 1) + j * SL
        frs[:, cols] = jnp.where(col_ids <= row_ids, frs[:, cols].astype(F32), 0.0).astype(BF)
        return 0

    lax.fori_loop(0, NF, lower, 0)
    for k in range(1, NF):

        @pl.when(f >= k)
        def _(k=k):
            p = f - k
            land(rhs_all.at[p], at_rhs + p)
            cols = pl.ds(pl.multiple_of(p * SH, 128), SH)
            y_acc[...] += dot_t(rhs_all[p], fac[:, cols])

    y_low = y_acc[...].astype(BF)

    load_cpl.wait()
    at = take(NF)
    for k in ORDER + (0,):
        p = turn(f, k, NF)
        rows = pl.ds(pl.multiple_of(p * UPS, 128), UPS)
        piece = dot_t(y_low, cpl[rows, :]).astype(BF)
        if k:
            up_send[k] = piece
            push(up_send.at[k], up_recv.at[f], at + f, dev_f(p))
        else:
            up_recv[f] = piece

    @pl.when(f == z)
    def _():
        land_ring(rr_all, at_rr, f, NF)
        rr_sum[...] = sum(dot(rr_all[j], place(j)) for j in range(NF))

    @pl.when(f != z)
    def _():
        rr_sum[...] = jnp.zeros_like(rr_sum)

    land_ring(up_recv, at, f, NF)
    up_all[f] = sum(up_recv[j].astype(F32) for j in range(NF)).astype(BF)
    at = take(NF)
    for k in ORDER:
        push(up_all.at[f], up_all.at[f], at + f, dev_f(turn(f, k, NF)))

    land_ring(up_all, at, f, NF)

    at_frt = take(NF)
    my_rows = pl.ds(pl.multiple_of(f * RR, 16), RR)
    for k in range(1, NF):
        p = turn(f, k, NF)
        cols = pl.ds(pl.multiple_of(p * SL, 128), SL)
        push(frs.at[:, cols], frt.at[my_rows], at_frt + f, dev_f(p))
    frt[my_rows, :] = frs[:, pl.ds(pl.multiple_of(f * SL, 128), SL)]

    adds = lax.rem(z + y + c, 2) == 0
    spot_mine = 2 * z + lax.div(y, 2)

    def leaf_sum(chunk, send, recv, full):
        at_sum = take(1)
        at_full = take(1)
        for turn_q in (2, 1, 3, 0):
            q = turn(lax.div(z, 2), turn_q, NY)
            send[q] = chunk(q).astype(BF).reshape(NS, N // NS, GR)
            for s in range(NS):
                zi = 2 * q + s // 2
                to = zi * NY + 2 * (s % 2) + lax.rem(zi + c, 2)
                slot = lax.rem(g - to + NG - 1, NG)
                push(send.at[q, s], recv.at[slot], at_sum, (to, f), to != g)

        @pl.when(adds)
        def _():
            land(recv.at[pl.ds(0, NG - 1)], at_sum)
            q = lax.div(spot_mine, NS)
            total = send[q, lax.rem(spot_mine, NS)].astype(F32)
            for j in range(NG - 1):
                total += recv[j].astype(F32)
            full[spot_mine] = total.astype(BF)

        for k in sorted(range(1, NG), key=lambda k: -min(k, NG - k)):
            to = turn(g, k, NG)
            push(full.at[spot_mine], full.at[spot_mine], at_full, (to, f), adds)

        @pl.when(adds)
        def _():
            land(full.at[pl.ds(0, NR - 1)], at_full)

        @pl.when(jnp.logical_not(adds))
        def _():
            land(full, at_full)

        parts = [full[pl.ds(NS * j, NS)].reshape(N, GR) for j in range(NY)]
        return jnp.concatenate(parts, axis=1)

    up_low = jnp.concatenate([up_all[j] for j in range(NF)], axis=1)

    def scatter_chunk(q):
        total = dot_t(up_low, onehot[pl.ds(pl.multiple_of(q * GR, 128), GR), :])
        return jnp.where(q == y, rr_sum[...], 0.0) - total

    b_low = leaf_sum(scatter_chunk, d_send, d_recv, d_all)

    land_ring_rows = [turn(f, NF - k, NF) for k in range(1, NF)]
    for p in land_ring_rows:
        land(frt.at[pl.ds(pl.multiple_of(p * RR, 16), RR)], at_frt + p)
    yr_send[...] = dot_t(b_low, frt[...]).astype(BF)
    at = take(1)
    push(yr_send, yr_sib, at, dev_f(x * NC + other))
    land(yr_sib, at)
    yr_all[x] = (yr_send[...].astype(F32) + yr_sib[...].astype(F32)).astype(BF)
    at = take(NX)
    for k in (2, 1, 3):
        push(yr_all.at[x], yr_all.at[x], at + x, dev_x(turn(x, k, NX)))
    land_ring(yr_all, at, x, NX)
    yr_low = sum(yr_all[j].astype(F32) for j in range(NX)).astype(BF)

    def back_chunk(q):
        return dot(yr_low, frt[:, pl.ds(pl.multiple_of(q * GR, 128), GR)])

    x_low = leaf_sum(back_chunk, x_send, x_recv, x_all)

    at = take(NF)
    for k in ORDER + (0,):
        p = turn(f, k, NF)
        cols = pl.ds(pl.multiple_of(p * UPS, 128), UPS)
        piece = dot(x_low, onehot[:, cols]).astype(BF)
        if k:
            pk_send[k] = piece
            push(pk_send.at[k], pk_recv.at[f], at + f, dev_f(p))
        else:
            pk_recv[f] = piece
    at_xr = take(1)

    @pl.when(f == z)
    def _():
        block = x_all[pl.ds(pl.multiple_of(NS * y, NS), NS)].reshape(N, GR)
        for j in range(NF):
            xr_send[j] = dot_t(block, place(j)).astype(BF)
        xr_recv[...] = xr_send[f]

    for k in ORDER:
        p = turn(f, k, NF)
        push(xr_send.at[p], xr_recv, at_xr, dev_f(p), f == z)
    land_ring(pk_recv, at, f, NF)
    pk_all[f] = sum(pk_recv[j].astype(F32) for j in range(NF)).astype(BF)
    at = take(NF)
    for k in ORDER:
        push(pk_all.at[f], pk_all.at[f], at + f, dev_f(turn(f, k, NF)))
    for k in (0,) + ORDER[::-1]:
        p = turn(f, NF - k, NF)
        if k:
            land(pk_all.at[p], at + p)
        rows = pl.ds(pl.multiple_of(p * UPS, 128), UPS)
        y_acc[...] -= dot(pk_all[p], cpl[rows, :])
    t_low = y_acc[...].astype(BF)

    at = take(NX)
    for k in range(NX):
        used = (x >= k) if k else (c == 1)
        i = turn(x, NX - k, NX)

        @pl.when(used)
        def _(i=i):
            cols = pl.ds(pl.multiple_of((i * NC + other) * SH, 128), SH)
            xb_send[i] = dot(t_low, fac[:, cols]).astype(BF)

        push(xb_send.at[i], xb_recv.at[i], at + i, dev_f(x * NC + other), used)
    at_xs = take(NX)
    for k in (1, 2, 3, 0):
        used = x >= k
        i = turn(x, NX - k, NX)
        cols = pl.ds(pl.multiple_of((i * NC + c) * SH, 128), SH)
        if k:

            @pl.when(used)
            def _(i=i, cols=cols):
                part = dot(t_low, fac[:, cols])
                land(xb_recv.at[i], at + i)
                xs_send[i] = (part + xb_recv[i].astype(F32)).astype(BF)

            push(xs_send.at[i], xs_recv.at[x], at_xs + x, dev_x(i), used)
        else:
            xs_acc[...] = dot(t_low, fac[:, cols])

            @pl.when(c == 0)
            def _(i=i):
                land(xb_recv.at[i], at + i)
                xs_acc[...] += xb_recv[i].astype(F32)

    for k in range(1, NX):

        @pl.when(x + k < NX)
        def _(k=k):
            land(xs_recv.at[x + k], at_xs + x + k)
            xs_acc[...] += xs_recv[x + k].astype(F32)

    at_next = take(1)
    at_prev = take(1)
    xs_low = xs_acc[...].astype(BF)
    keep_sub = pltpu.make_async_copy(xs_acc, xs_hbm, lsem.at[11])
    keep_sub.start()
    if_send[0] = xs_low[:, SH - RIM :]
    push(if_send.at[0], if_recv.at[0], at_next, (turn(g, 1, NG), f))
    load_iface.wait()
    if_send[1] = dot(xs_low[:, :RIM], iface_ref[...]).astype(BF)
    push(if_send.at[1], if_recv.at[1], at_prev, (turn(g, NG - 1, NG), f))

    @pl.when(f != z)
    def _():
        land(xr_recv, at_xr)

    load_mroot.wait()
    xr_out[...] = dot_t(widen, xr_recv[...])
    keep_root = pltpu.make_async_copy(xr_out, xr_hbm, lsem.at[12])
    keep_root.start()
    mx_own = (xr_recv[...].astype(F32)[:, :RR] * mroot_in[...]).astype(BF)
    load_brt.wait()

    load_mass.wait()
    mass_x = xs_acc[...] * mass_ref[...]
    land(if_recv.at[0], at_next)
    first = mass_x[:, :RIM] + dot_t(if_recv[0], iface_ref[...])
    land(if_recv.at[1], at_prev)
    last = mass_x[:, SH - RIM :] + if_recv[1].astype(F32)
    mx = jnp.concatenate([first, last], axis=1).astype(BF)

    load_bas.wait()

    def gram_part(block):
        cols = pl.ds(pl.multiple_of(block * NBS, 128), NBS)
        return dot(mx, bas[:, cols]) + dot(mx_own, brt[:, cols])

    at = take(NX)
    for j in range(NX):
        gc_send[j] = gram_part(other * NX + j).astype(BF)
        push(gc_send.at[j], gc_recv.at[j], at + j, dev_f(x * NC + other))
    for j in range(NX):
        gc_own[j] = gram_part(c * NX + j)
    at_p = take(1)
    for i in (2, 1, 3, 0):
        xi = turn(x, i, NX)
        land(gc_recv.at[xi], at + xi)
        part = gc_own[xi] + gc_recv[xi].astype(F32)
        gp_send[xi] = part.astype(BF).reshape(NY, N // NY, NBS)
        for j in (2, 1, 3, 0):
            if i or j:
                yj = turn(y, j, NY)
                slot = ((NX - i) % NX) * NY + (NY - j) % NY - 1
                push(gp_send.at[xi, yj], gp_recv.at[slot], at_p, dev_xy(xi, yj))
    land(gp_recv, at_p)
    total = gp_send[x, y].astype(F32)
    for j in range(NX * NY - 1):
        total += gp_recv[j].astype(F32)
    gz_all[z] = total.astype(BF)
    at = take(NZ)
    for k in (4, 3, 5, 2, 6, 1, 7):
        push(gz_all.at[z], gz_all.at[z], at + z, dev_z(turn(z, k, NZ)))
    land_ring(gz_all, at, z, NZ)
    mine = c * NX + x
    g_all[mine, y] = sum(gz_all[j].astype(F32) for j in range(NZ)).astype(BF)
    at = take(1)
    for i in (2, 1, 3, 0):
        for j in (2, 1, 3, 0):
            if i or j:
                to = dev_xy(turn(x, i, NX), turn(y, j, NY))
                push(g_all.at[mine, y], g_all.at[mine, y], at, to)
    land(gp_recv, at)
    at = take(1)
    half = pl.ds(pl.multiple_of(c * NX, NX), NX)
    push(g_all.at[half], g_all.at[half], at, dev_f(x * NC + other))

    keep_mine = pltpu.make_async_copy(g_all.at[half], g_hbm.at[half], lsem.at[13])
    keep_mine.start()
    rest = pl.ds(pl.multiple_of(other * NX, NX), NX)
    land(g_all.at[rest], at)
    keep_rest = pltpu.make_async_copy(g_all.at[rest], g_hbm.at[rest], lsem.at[14])
    keep_rest.start()

    for copy, cond in sends:
        if cond is None:
            copy.wait_send()
        else:
            pl.when(cond)(copy.wait_send)
    for keep in (keep_sub, keep_root, keep_mine, keep_rest):
        keep.wait()


def finish(xs_ref, xr_ref, g_ref, bas_ref, brt_ref, new_sub_ref, new_root_ref, gram_ref):
    @pl.when(pl.program_id(0) == 0)
    def _():
        new_sub_ref[...] = xs_ref[...]
        new_root_ref[...] = xr_ref[...]

    for j in range(STEP):
        cols = pl.ds(j * NBS, NBS)
        low = g_ref[j].reshape(N, NBS)
        gram_ref[:, cols] = low.astype(F32)
        new_sub_ref[...] -= dot_t(low, bas_ref[:, cols])
        new_root_ref[...] -= dot_t(brt_ref[:, cols], low)


def body(
    rhs_sub,
    rhs_root,
    factor_sub,
    coupling,
    update_rows,
    factor_root,
    mass_sub,
    mass_root,
    interface,
    basis_sub,
    basis_root,
):
    hbm = pl.BlockSpec(memory_space=pl.ANY)
    leaf_sum = [
        pltpu.VMEM((NY, NS, N // NS, GR), BF),
        pltpu.VMEM((NG, N // NS, GR), BF),
        pltpu.VMEM((NR, N // NS, GR), BF),
    ]
    xs, xr, low = pl.pallas_call(
        kernel,
        out_shape=(
            jax.ShapeDtypeStruct((N, SH), F32),
            jax.ShapeDtypeStruct((RR, N), F32),
            jax.ShapeDtypeStruct((NF, NY, N // NY, NBS), BF),
        ),
        in_specs=[hbm] * 11,
        out_specs=(hbm, hbm, hbm),
        scratch_shapes=[
            pltpu.VMEM((N, SH), F32),
            pltpu.VMEM((RR, N), F32),
            pltpu.VMEM((SH, SUB), BF),
            pltpu.VMEM((UP, SH), BF),
            pltpu.VMEM((1, UP), jnp.int32),
            pltpu.VMEM((RR, ROOT), BF),
            pltpu.VMEM((1, SH), F32),
            pltpu.VMEM((1, RR), F32),
            pltpu.VMEM((RIM, RIM), BF),
            pltpu.VMEM((SH, NB), BF),
            pltpu.VMEM((RR, NB), BF),
            pltpu.VMEM((SL, UP), BF),
            pltpu.VMEM((GR, SL), BF),
            pltpu.VMEM((NF, N, SH), BF),
            pltpu.VMEM((N, PAD), BF),
            pltpu.VMEM((NF, N, PAD), BF),
            pltpu.VMEM((N, GR), F32),
            pltpu.VMEM((N, SH), F32),
            pltpu.VMEM((NF, N, UPS), BF),
            pltpu.VMEM((NF, N, UPS), BF),
            pltpu.VMEM((NF, N, UPS), BF),
            *leaf_sum,
            pltpu.VMEM((N, GR), BF),
            pltpu.VMEM((N, GR), BF),
            pltpu.VMEM((NX, N, GR), BF),
            *leaf_sum,
            pltpu.VMEM((NF, N, PAD), BF),
            pltpu.VMEM((N, PAD), BF),
            pltpu.VMEM((NF, N, UPS), BF),
            pltpu.VMEM((NF, N, UPS), BF),
            pltpu.VMEM((NF, N, UPS), BF),
            pltpu.VMEM((NX, N, SH), BF),
            pltpu.VMEM((NX, N, SH), BF),
            pltpu.VMEM((NX, N, SH), BF),
            pltpu.VMEM((NX, N, SH), BF),
            pltpu.VMEM((N, SH), F32),
            pltpu.VMEM((RR, N), F32),
            pltpu.VMEM((2, N, RIM), BF),
            pltpu.VMEM((2, N, RIM), BF),
            pltpu.VMEM((NX, N, NBS), BF),
            pltpu.VMEM((NX, N, NBS), BF),
            pltpu.VMEM((NX, N, NBS), F32),
            pltpu.VMEM((NX, NY, N // NY, NBS), BF),
            pltpu.VMEM((NX * NY - 1, N // NY, NBS), BF),
            pltpu.VMEM((NZ, N // NY, NBS), BF),
            pltpu.VMEM((NF, NY, N // NY, NBS), BF),
            pltpu.SemaphoreType.DMA((SENDS,)),
            pltpu.SemaphoreType.DMA((RECVS,)),
            pltpu.SemaphoreType.DMA((16,)),
        ],
        compiler_params=pltpu.CompilerParams(
            collective_id=0, has_side_effects=True, vmem_limit_bytes=56 * 1024 * 1024
        ),
    )(
        rhs_sub.T,
        rhs_root,
        factor_sub[0],
        coupling[0],
        update_rows,
        factor_root,
        mass_sub[None, :],
        mass_root[None, :],
        interface[0],
        basis_sub,
        basis_root,
    )
    whole = pl.BlockSpec((N, SH), lambda i: (0, 0))
    root = pl.BlockSpec((RR, N), lambda i: (0, 0))
    new_sub, new_root, gram = pl.pallas_call(
        finish,
        grid=(NF // STEP,),
        out_shape=(
            jax.ShapeDtypeStruct((N, SH), F32),
            jax.ShapeDtypeStruct((RR, N), F32),
            jax.ShapeDtypeStruct((N, NB), F32),
        ),
        in_specs=[
            whole,
            root,
            pl.BlockSpec((STEP, NY, N // NY, NBS), lambda i: (i, 0, 0, 0)),
            pl.BlockSpec((SH, STEP * NBS), lambda i: (0, i)),
            pl.BlockSpec((RR, STEP * NBS), lambda i: (0, i)),
        ],
        out_specs=(whole, root, pl.BlockSpec((N, STEP * NBS), lambda i: (0, i))),
    )(xs, xr, low, basis_sub, basis_root)
    return new_sub.T, new_root, gram.T


def solution(mesh):
    placed = (
        P(("leaf", "front"), None),
        P(("leaf", "front"), None),
        P("leaf", "front", None),
        P("leaf", None, "front"),
        P("leaf", None),
        P(("leaf", "front"), None),
        P(("leaf", "front")),
        P(("leaf", "front")),
        P(("leaf", "front"), None, None),
        P(("leaf", "front"), None),
        P(("leaf", "front"), None),
    )
    return jax.shard_map(
        body,
        mesh=mesh,
        in_specs=placed,
        out_specs=(P(("leaf", "front"), None), P(("leaf", "front"), None), P()),
        check_vma=False,
    )
```

```python
import jax
import jax.numpy as jnp
from jax import lax
from jax.experimental import pallas as pl
from jax.experimental.pallas import tpu as pltpu
from jax.sharding import PartitionSpec as P

BF = jnp.bfloat16
F32 = jnp.float32
MESH = pl.DeviceIdType.MESH

N = 64
NF = 8
NY = 4
NZ = 8
NX = 4
NC = 2
NG = NY * NZ
NS = 4
NR = NY * NS
SH = 512
SUB = NF * SH
UP = 2048
UPS = UP // NF
RR = 48
GR = NF * RR
SL = NY * GR
ROOT = NF * SL
RIM = 256
NB = 2048
NBS = NB // NF
PAD = 128
STEP = 8
ORDER = (4, 5, 3, 2, 6, 7, 1)
SENDS = 240
RECVS = 160


def dot(a, b):
    return jnp.dot(a, b, preferred_element_type=F32)


def dot_t(a, b):
    return lax.dot_general(a, b, (((1,), (1,)), ((), ())), preferred_element_type=F32)


def kernel(
    rhs_hbm,
    rroot_hbm,
    factor_hbm,
    coupling_hbm,
    rows_hbm,
    froot_hbm,
    mass_hbm,
    mroot_hbm,
    iface_hbm,
    basis_hbm,
    broot_hbm,
    xs_hbm,
    xr_hbm,
    g_hbm,
    rhs_in,
    rroot_in,
    fac,
    cpl,
    rows_ref,
    frs,
    mass_ref,
    mroot_in,
    iface_ref,
    bas,
    brt,
    onehot,
    frt,
    rhs_all,
    rr_send,
    rr_all,
    rr_sum,
    y_acc,
    up_send,
    up_recv,
    up_all,
    d_send,
    d_recv,
    d_all,
    yr_send,
    yr_sib,
    yr_all,
    x_send,
    x_recv,
    x_all,
    x_sum,
    xr_send,
    xr_recv,
    pk_send,
    pk_recv,
    pk_all,
    xb_send,
    xb_recv,
    xs_send,
    xs_recv,
    xs_acc,
    xr_out,
    if_send,
    if_recv,
    gc_send,
    gc_recv,
    gc_own,
    gp_send,
    gp_recv,
    gz_all,
    g_all,
    ssem,
    rsem,
    lsem,
):
    g = lax.axis_index("leaf")
    f = lax.axis_index("front")
    z = lax.div(g, NY)
    y = lax.rem(g, NY)
    x = lax.div(f, NC)
    c = lax.rem(f, NC)
    other = 1 - c

    def slice_of(i):
        half = lax.div(i, NC)
        return jnp.where(lax.rem(i, NC) == 0, half, NF - 1 - half)

    def holder_of(i):
        return jnp.where(i < NX, NC * i, NC * (NF - 1 - i) + 1)

    part = slice_of(f)
    reached = z >= part

    def dev_f(i):
        return (g, i)

    def dev_x(i):
        return (g, i * NC + c)

    def dev_z(i):
        return (i * NY + y, f)

    def dev_xy(i, j):
        return (z * NY + j, i * NC + c)

    def turn(a, k, n):
        return lax.rem(a + k, n)

    loads = [
        (rhs_hbm, rhs_in),
        (rroot_hbm, rroot_in),
        (rows_hbm, rows_ref),
        (factor_hbm, fac),
        (froot_hbm, frs),
        (coupling_hbm, cpl),
        (iface_hbm, iface_ref),
        (mass_hbm, mass_ref),
        (mroot_hbm, mroot_in),
        (broot_hbm, brt),
        (basis_hbm, bas),
    ]
    loads = [pltpu.make_async_copy(a, b, lsem.at[i]) for i, (a, b) in enumerate(loads)]
    (
        load_rhs,
        load_rroot,
        load_rows,
        load_fac,
        load_frs,
        load_cpl,
        load_iface,
        load_mass,
        load_mroot,
        load_brt,
        load_bas,
    ) = loads
    barrier = pltpu.get_barrier_semaphore()
    def hops(k, n):
        return min(k, n - k)

    peers = [(hops(i, NX), (g, turn(x, i, NX) * NC + c)) for i in range(1, NX)]
    peers += [(hops(i, NX), (g, turn(x, i, NX) * NC + other)) for i in range(NX)]
    peers += [
        (hops(j, NY) + hops(i, NZ), (turn(z, i, NZ) * NY + turn(y, j, NY), f))
        for i in range(NZ)
        for j in range(NY)
        if i or j
    ]
    peers += [
        (hops(i, NX) + hops(j, NY), dev_xy(turn(x, i, NX), turn(y, j, NY)))
        for i in range(1, NX)
        for j in range(1, NY)
    ]
    for _, dev in sorted(peers, key=lambda peer: -peer[0]):
        pl.semaphore_signal(barrier, inc=1, device_id=dev, device_id_type=MESH)
    for load in loads:
        load.start()

    sends = []
    later = []
    slots = [0]
    sent = [0]

    def take(n):
        slots[0] += n
        assert slots[0] <= RECVS
        return slots[0] - n

    def push(src, dst, slot, dev, cond=None, to=sends):
        assert sent[0] < SENDS
        copy = pltpu.make_async_remote_copy(
            src_ref=src,
            dst_ref=dst,
            send_sem=ssem.at[sent[0]],
            recv_sem=rsem.at[slot],
            device_id=dev,
            device_id_type=MESH,
        )
        sent[0] += 1
        if cond is None:
            copy.start()
        else:
            pl.when(cond)(copy.start)
        to.append((copy, cond))

    def settle(keep, of=sends):
        done = of[: len(of) - keep]
        del of[: len(of) - keep]
        while done:
            cond = done[0][1]
            same = [copy for copy, other_cond in done if other_cond is cond]
            done = [pair for pair in done if pair[1] is not cond]

            def wait(same=same):
                for copy in same:
                    copy.wait_send()

            if cond is None:
                wait()
            else:
                pl.when(cond)(wait)

    def land(buf, slot):
        pltpu.make_async_remote_copy(
            src_ref=buf,
            dst_ref=buf,
            send_sem=ssem.at[0],
            recv_sem=rsem.at[slot],
            device_id=(g, f),
            device_id_type=MESH,
        ).wait_recv()

    def land_ring(buf, base, me, n):
        for k in range(1, n):
            p = turn(me, n - k, n)
            land(buf.at[p], base + p)

    spot = lax.broadcasted_iota(jnp.int32, (PAD, GR), 0)
    lane = lax.broadcasted_iota(jnp.int32, (PAD, GR), 1)

    def place(j):
        return jnp.where((lane == spot + j * RR) & (spot < RR), 1.0, 0.0).astype(BF)

    widen = jnp.where(
        lax.broadcasted_iota(jnp.int32, (RR, PAD), 0)
        == lax.broadcasted_iota(jnp.int32, (RR, PAD), 1),
        1.0,
        0.0,
    ).astype(BF)
    unit = jnp.where(
        lax.broadcasted_iota(jnp.int32, (N, N), 0) == lax.broadcasted_iota(jnp.int32, (N, N), 1),
        1.0,
        0.0,
    ).astype(BF)
    load_rhs.wait()
    rhs_all[f] = rhs_in[...].astype(BF)
    load_rroot.wait()
    rr_mine = dot(dot_t(unit, rroot_in[...].astype(BF)).astype(BF), widen).astype(BF)
    rr_send[...] = rr_mine
    rr_all[f] = rr_mine

    pl.semaphore_wait(barrier, len(peers))

    at = take(NF)
    for k in range(1, NF):
        push(rhs_all.at[f], rhs_all.at[f], at + f, dev_f(turn(f, k, NF)), f + k < NF)
    at_rhs = at
    at_rr = take(NF)
    push(rr_send, rr_all.at[f], at_rr + f, dev_f(holder_of(z)), part != z)

    load_rows.wait()

    def hot(i, _):
        rows = pl.ds(pl.multiple_of(i * 64, 64), 64)
        ids = lax.broadcasted_iota(jnp.int32, (64, UP), 0) + (part * SL + i * 64)
        onehot[rows, :] = jnp.where(ids == rows_ref[...], 1.0, 0.0).astype(BF)
        return 0

    lax.fori_loop(0, SL // 64, hot, 0)

    load_fac.wait()
    mine = pl.ds(pl.multiple_of(f * SH, 128), SH)
    below = lax.broadcasted_iota(jnp.int32, (SH, SH), 1) <= lax.broadcasted_iota(
        jnp.int32, (SH, SH), 0
    )
    diag = jnp.where(below, fac[:, mine].astype(F32), 0.0).astype(BF)
    fac[:, mine] = diag
    y_acc[...] = dot_t(rhs_all[f], diag)

    load_frs.wait()

    def lower(j, _):
        cols = pl.ds(pl.multiple_of(j * SL, 128), SL)
        row_ids = lax.broadcasted_iota(jnp.int32, (RR, SL), 0) + (g * GR + f * RR)
        col_ids = lax.broadcasted_iota(jnp.int32, (RR, SL), 1) + j * SL
        frs[:, cols] = jnp.where(col_ids <= row_ids, frs[:, cols].astype(F32), 0.0).astype(BF)
        return 0

    lax.fori_loop(0, NF, lower, 0)
    for k in range(1, NF):

        @pl.when(f >= k)
        def _(k=k):
            p = f - k
            land(rhs_all.at[p], at_rhs + p)
            cols = pl.ds(pl.multiple_of(p * SH, 128), SH)
            y_acc[...] += dot_t(rhs_all[p], fac[:, cols])

    y_low = y_acc[...].astype(BF)

    load_cpl.wait()
    at = take(NF)
    for k in ORDER + (0,):
        p = turn(f, k, NF)
        rows = pl.ds(pl.multiple_of(p * UPS, 128), UPS)
        piece = dot_t(y_low, cpl[rows, :]).astype(BF)
        if k:
            up_send[k] = piece
            push(up_send.at[k], up_recv.at[f], at + f, dev_f(p))
        else:
            up_recv[f] = piece
    settle(NF - 1)

    @pl.when(part == z)
    def _():
        land_ring(rr_all, at_rr, f, NF)
        rr_sum[...] = sum(dot(rr_all[j], place(j)) for j in range(NF))

    @pl.when(part != z)
    def _():
        rr_sum[...] = jnp.zeros_like(rr_sum)

    land_ring(up_recv, at, f, NF)
    up_all[f] = sum(up_recv[j].astype(F32) for j in range(NF)).astype(BF)
    at = take(NF)
    for k in ORDER:
        push(up_all.at[f], up_all.at[f], at + f, dev_f(turn(f, k, NF)))

    land_ring(up_all, at, f, NF)

    at_frt = take(NF)
    my_rows = pl.ds(pl.multiple_of(f * RR, 16), RR)
    for k in range(1, NF):
        p = turn(f, k, NF)
        to = slice_of(p)
        cols = pl.ds(pl.multiple_of(to * SL, 128), SL)
        push(frs.at[:, cols], frt.at[my_rows], at_frt + f, dev_f(p), to <= z, later)
    frt[my_rows, :] = frs[:, pl.ds(pl.multiple_of(part * SL, 128), SL)]

    adds = lax.rem(z + y + c, 2) == 0
    spot_mine = 2 * z + lax.div(y, 2)

    def cut(chunk, q, send):
        send[q] = chunk(q).astype(BF).reshape(NS, N // NS, GR)

    def hand_out(q, send, recv, slot_of, at, cond=None):
        for i in range(NS):
            zi = 2 * q + i // 2
            to = zi * NY + 2 * (i % 2) + lax.rem(zi + c, 2)
            use = to != g if cond is None else cond & (to != g)
            push(send.at[q, i], recv.at[slot_of(to)], at, (to, f), use)

    def own_piece(send):
        return send[lax.div(spot_mine, NS), lax.rem(spot_mine, NS)]

    def hand_back(full, some):
        at = take(1)
        for k in sorted(range(1, NG), key=lambda k: -min(k, NG - k)):
            to = turn(g, k, NG)
            use = adds & (lax.div(to, NY) >= part) if some else adds
            push(full.at[spot_mine], full.at[spot_mine], at, (to, f), use)
        wanted = reached if some else part >= 0

        @pl.when(adds & wanted)
        def _():
            land(full.at[pl.ds(0, NR - 1)], at)

        @pl.when(jnp.logical_not(adds) & wanted)
        def _():
            land(full, at)

        parts = [full[pl.ds(NS * j, NS)].reshape(N, GR) for j in range(NY)]
        return jnp.concatenate(parts, axis=1)

    up_low = jnp.concatenate([up_all[j] for j in range(NF)], axis=1)

    def scatter_chunk(q):
        total = dot_t(up_low, onehot[pl.ds(pl.multiple_of(q * GR, 128), GR), :])
        return jnp.where(q == y, rr_sum[...], 0.0) - total

    at = take(1)
    for k in (2, 1, 3, 0):
        q = turn(lax.div(z, 2), k, NY)
        cut(scatter_chunk, q, d_send)
        hand_out(q, d_send, d_recv, lambda to: lax.rem(g - to + NG - 1, NG), at)
    settle(NR)

    @pl.when(adds)
    def _():
        land(d_recv.at[pl.ds(0, NG - 1)], at)
        total = own_piece(d_send).astype(F32)
        for j in range(NG - 1):
            total += d_recv[j].astype(F32)
        d_all[spot_mine] = total.astype(BF)

    b_low = hand_back(d_all, True)

    @pl.when(reached)
    def _():
        for k in range(1, NF):
            p = turn(f, NF - k, NF)
            land(frt.at[pl.ds(pl.multiple_of(p * RR, 16), RR)], at_frt + p)
        yr_send[...] = dot_t(b_low, frt[...]).astype(BF)

    @pl.when(jnp.logical_not(reached))
    def _():
        yr_send[...] = jnp.zeros_like(yr_send)

    at = take(1)
    push(yr_send, yr_sib, at, dev_f(x * NC + other))
    land(yr_sib, at)
    yr_all[x] = (yr_send[...].astype(F32) + yr_sib[...].astype(F32)).astype(BF)
    at = take(NX)
    for k in (2, 1, 3):
        push(yr_all.at[x], yr_all.at[x], at + x, dev_x(turn(x, k, NX)))
    settle(NX - 1)
    land_ring(yr_all, at, x, NX)
    yr_low = sum(yr_all[j].astype(F32) for j in range(NX)).astype(BF)

    def back_chunk(q):
        return dot(yr_low, frt[:, pl.ds(pl.multiple_of(q * GR, 128), GR)])

    at = take(NZ)
    for k in (2, 1, 3, 0):
        q = turn(lax.div(z, 2), k, NY)

        @pl.when(reached)
        def _(q=q):
            cut(back_chunk, q, x_send)

        hand_out(q, x_send, x_recv, lambda to: g, at + z, reached)
    settle(NR)

    @pl.when(adds)
    def _():
        x_sum[...] = jnp.zeros_like(x_sum)

        @pl.when(reached)
        def _():
            x_recv[g] = own_piece(x_send)

        for i in range(NZ):

            @pl.when(i >= part)
            def _(i=i):
                @pl.when(z == i)
                def _():
                    land(x_recv.at[pl.ds(NY * i, NY - 1)], at + i)

                @pl.when(z != i)
                def _():
                    land(x_recv.at[pl.ds(NY * i, NY)], at + i)

                x_sum[...] += sum(x_recv[NY * i + j].astype(F32) for j in range(NY))

        x_all[spot_mine] = x_sum[...].astype(BF)

    x_low = hand_back(x_all, False)

    at = take(NF)
    for k in ORDER + (0,):
        p = turn(f, k, NF)
        cols = pl.ds(pl.multiple_of(p * UPS, 128), UPS)
        piece = dot(x_low, onehot[:, cols]).astype(BF)
        if k:
            pk_send[k] = piece
            push(pk_send.at[k], pk_recv.at[f], at + f, dev_f(p))
        else:
            pk_recv[f] = piece
    at_xr = take(1)

    @pl.when(part == z)
    def _():
        block = x_all[pl.ds(pl.multiple_of(NS * y, NS), NS)].reshape(N, GR)
        for j in range(NF):
            xr_send[j] = dot_t(block, place(j)).astype(BF)
        xr_recv[...] = xr_send[f]

    for k in ORDER:
        p = turn(f, k, NF)
        push(xr_send.at[p], xr_recv, at_xr, dev_f(p), part == z)
    settle(2 * NF - 2)
    settle(0, later)
    land_ring(pk_recv, at, f, NF)
    pk_all[f] = sum(pk_recv[j].astype(F32) for j in range(NF)).astype(BF)
    at = take(NF)
    for k in ORDER:
        push(pk_all.at[f], pk_all.at[f], at + f, dev_f(turn(f, k, NF)))
    for k in (0,) + ORDER[::-1]:
        p = turn(f, NF - k, NF)
        if k:
            land(pk_all.at[p], at + p)
        rows = pl.ds(pl.multiple_of(p * UPS, 128), UPS)
        y_acc[...] -= dot(pk_all[p], cpl[rows, :])
    t_low = y_acc[...].astype(BF)

    at = take(NX)
    for k in range(NX):
        used = (x >= k) if k else (c == 1)
        i = turn(x, NX - k, NX)

        @pl.when(used)
        def _(i=i):
            cols = pl.ds(pl.multiple_of((i * NC + other) * SH, 128), SH)
            xb_send[i] = dot(t_low, fac[:, cols]).astype(BF)

        push(xb_send.at[i], xb_recv.at[i], at + i, dev_f(x * NC + other), used)
    at_xs = take(NX)
    for k in (1, 2, 3, 0):
        used = x >= k
        i = turn(x, NX - k, NX)
        cols = pl.ds(pl.multiple_of((i * NC + c) * SH, 128), SH)
        if k:

            @pl.when(used)
            def _(i=i, cols=cols):
                part = dot(t_low, fac[:, cols])
                land(xb_recv.at[i], at + i)
                xs_send[i] = (part + xb_recv[i].astype(F32)).astype(BF)

            push(xs_send.at[i], xs_recv.at[x], at_xs + x, dev_x(i), used)
        else:
            xs_acc[...] = dot(t_low, fac[:, cols])

            @pl.when(c == 0)
            def _(i=i):
                land(xb_recv.at[i], at + i)
                xs_acc[...] += xb_recv[i].astype(F32)

    for k in range(1, NX):

        @pl.when(x + k < NX)
        def _(k=k):
            land(xs_recv.at[x + k], at_xs + x + k)
            xs_acc[...] += xs_recv[x + k].astype(F32)

    at_next = take(1)
    at_prev = take(1)
    xs_low = xs_acc[...].astype(BF)
    keep_sub = pltpu.make_async_copy(xs_acc, xs_hbm, lsem.at[11])
    keep_sub.start()
    if_send[0] = xs_low[:, SH - RIM :]
    push(if_send.at[0], if_recv.at[0], at_next, (turn(g, 1, NG), f))
    load_iface.wait()
    if_send[1] = dot(xs_low[:, :RIM], iface_ref[...]).astype(BF)
    push(if_send.at[1], if_recv.at[1], at_prev, (turn(g, NG - 1, NG), f))

    settle(2)

    @pl.when(part != z)
    def _():
        land(xr_recv, at_xr)

    load_mroot.wait()
    xr_out[...] = dot_t(widen, xr_recv[...])
    keep_root = pltpu.make_async_copy(xr_out, xr_hbm, lsem.at[12])
    keep_root.start()
    mx_own = (xr_recv[...].astype(F32)[:, :RR] * mroot_in[...]).astype(BF)
    load_brt.wait()

    load_mass.wait()
    mass_x = xs_acc[...] * mass_ref[...]
    land(if_recv.at[0], at_next)
    first = mass_x[:, :RIM] + dot_t(if_recv[0], iface_ref[...])
    land(if_recv.at[1], at_prev)
    last = mass_x[:, SH - RIM :] + if_recv[1].astype(F32)
    mx = jnp.concatenate([first, last], axis=1).astype(BF)

    load_bas.wait()

    def gram_part(block):
        cols = pl.ds(pl.multiple_of(block * NBS, 128), NBS)
        return dot(mx, bas[:, cols]) + dot(mx_own, brt[:, cols])

    at = take(NX)
    for j in range(NX):
        gc_send[j] = gram_part(other * NX + j).astype(BF)
        push(gc_send.at[j], gc_recv.at[j], at + j, dev_f(x * NC + other))
    for j in range(NX):
        gc_own[j] = gram_part(c * NX + j)
    at_p = take(1)
    for i in (2, 1, 3, 0):
        xi = turn(x, i, NX)
        land(gc_recv.at[xi], at + xi)
        pair = gc_own[xi] + gc_recv[xi].astype(F32)
        gp_send[xi] = pair.astype(BF).reshape(NY, N // NY, NBS)
        for j in (2, 1, 3, 0):
            if i or j:
                yj = turn(y, j, NY)
                slot = ((NX - i) % NX) * NY + (NY - j) % NY - 1
                push(gp_send.at[xi, yj], gp_recv.at[slot], at_p, dev_xy(xi, yj))
    settle(NX * NY - 1)
    land(gp_recv, at_p)
    total = gp_send[x, y].astype(F32)
    for j in range(NX * NY - 1):
        total += gp_recv[j].astype(F32)
    gz_all[z] = total.astype(BF)
    at = take(NZ)
    for k in (4, 3, 5, 2, 6, 1, 7):
        push(gz_all.at[z], gz_all.at[z], at + z, dev_z(turn(z, k, NZ)))
    settle(NZ - 1)
    land_ring(gz_all, at, z, NZ)
    mine = c * NX + x
    g_all[mine, y] = sum(gz_all[j].astype(F32) for j in range(NZ)).astype(BF)
    at = take(1)
    for i in (2, 1, 3, 0):
        for j in (2, 1, 3, 0):
            if i or j:
                to = dev_xy(turn(x, i, NX), turn(y, j, NY))
                push(g_all.at[mine, y], g_all.at[mine, y], at, to)
    settle(NX * NY - 1)
    land(gp_recv, at)
    at = take(1)
    half = pl.ds(pl.multiple_of(c * NX, NX), NX)
    push(g_all.at[half], g_all.at[half], at, dev_f(x * NC + other))

    keep_mine = pltpu.make_async_copy(g_all.at[half], g_hbm.at[half], lsem.at[13])
    keep_mine.start()
    settle(1)
    rest = pl.ds(pl.multiple_of(other * NX, NX), NX)
    land(g_all.at[rest], at)
    keep_rest = pltpu.make_async_copy(g_all.at[rest], g_hbm.at[rest], lsem.at[14])
    keep_rest.start()

    settle(0)
    for keep in (keep_sub, keep_root, keep_mine, keep_rest):
        keep.wait()


def finish(xs_ref, xr_ref, g_ref, bas_ref, brt_ref, new_sub_ref, new_root_ref, gram_ref):
    @pl.when(pl.program_id(0) == 0)
    def _():
        new_sub_ref[...] = xs_ref[...]
        new_root_ref[...] = xr_ref[...]

    for j in range(STEP):
        cols = pl.ds(j * NBS, NBS)
        low = g_ref[j].reshape(N, NBS)
        gram_ref[:, cols] = low.astype(F32)
        new_sub_ref[...] -= dot_t(low, bas_ref[:, cols])
        new_root_ref[...] -= dot_t(brt_ref[:, cols], low)


def body(
    rhs_sub,
    rhs_root,
    factor_sub,
    coupling,
    update_rows,
    factor_root,
    mass_sub,
    mass_root,
    interface,
    basis_sub,
    basis_root,
):
    hbm = pl.BlockSpec(memory_space=pl.ANY)
    leaf_sum = [
        pltpu.VMEM((NY, NS, N // NS, GR), BF),
        pltpu.VMEM((NG, N // NS, GR), BF),
        pltpu.VMEM((NR, N // NS, GR), BF),
    ]
    xs, xr, low = pl.pallas_call(
        kernel,
        out_shape=(
            jax.ShapeDtypeStruct((N, SH), F32),
            jax.ShapeDtypeStruct((RR, N), F32),
            jax.ShapeDtypeStruct((NF, NY, N // NY, NBS), BF),
        ),
        in_specs=[hbm] * 11,
        out_specs=(hbm, hbm, hbm),
        scratch_shapes=[
            pltpu.VMEM((N, SH), F32),
            pltpu.VMEM((RR, N), F32),
            pltpu.VMEM((SH, SUB), BF),
            pltpu.VMEM((UP, SH), BF),
            pltpu.VMEM((1, UP), jnp.int32),
            pltpu.VMEM((RR, ROOT), BF),
            pltpu.VMEM((1, SH), F32),
            pltpu.VMEM((1, RR), F32),
            pltpu.VMEM((RIM, RIM), BF),
            pltpu.VMEM((SH, NB), BF),
            pltpu.VMEM((RR, NB), BF),
            pltpu.VMEM((SL, UP), BF),
            pltpu.VMEM((GR, SL), BF),
            pltpu.VMEM((NF, N, SH), BF),
            pltpu.VMEM((N, PAD), BF),
            pltpu.VMEM((NF, N, PAD), BF),
            pltpu.VMEM((N, GR), F32),
            pltpu.VMEM((N, SH), F32),
            pltpu.VMEM((NF, N, UPS), BF),
            pltpu.VMEM((NF, N, UPS), BF),
            pltpu.VMEM((NF, N, UPS), BF),
            *leaf_sum,
            pltpu.VMEM((N, GR), BF),
            pltpu.VMEM((N, GR), BF),
            pltpu.VMEM((NX, N, GR), BF),
            *leaf_sum,
            pltpu.VMEM((N // NS, GR), F32),
            pltpu.VMEM((NF, N, PAD), BF),
            pltpu.VMEM((N, PAD), BF),
            pltpu.VMEM((NF, N, UPS), BF),
            pltpu.VMEM((NF, N, UPS), BF),
            pltpu.VMEM((NF, N, UPS), BF),
            pltpu.VMEM((NX, N, SH), BF),
            pltpu.VMEM((NX, N, SH), BF),
            pltpu.VMEM((NX, N, SH), BF),
            pltpu.VMEM((NX, N, SH), BF),
            pltpu.VMEM((N, SH), F32),
            pltpu.VMEM((RR, N), F32),
            pltpu.VMEM((2, N, RIM), BF),
            pltpu.VMEM((2, N, RIM), BF),
            pltpu.VMEM((NX, N, NBS), BF),
            pltpu.VMEM((NX, N, NBS), BF),
            pltpu.VMEM((NX, N, NBS), F32),
            pltpu.VMEM((NX, NY, N // NY, NBS), BF),
            pltpu.VMEM((NX * NY - 1, N // NY, NBS), BF),
            pltpu.VMEM((NZ, N // NY, NBS), BF),
            pltpu.VMEM((NF, NY, N // NY, NBS), BF),
            pltpu.SemaphoreType.DMA((SENDS,)),
            pltpu.SemaphoreType.DMA((RECVS,)),
            pltpu.SemaphoreType.DMA((16,)),
        ],
        compiler_params=pltpu.CompilerParams(
            collective_id=0, has_side_effects=True, vmem_limit_bytes=56 * 1024 * 1024
        ),
    )(
        rhs_sub.T,
        rhs_root,
        factor_sub[0],
        coupling[0],
        update_rows,
        factor_root,
        mass_sub[None, :],
        mass_root[None, :],
        interface[0],
        basis_sub,
        basis_root,
    )
    whole = pl.BlockSpec((N, SH), lambda i: (0, 0))
    root = pl.BlockSpec((RR, N), lambda i: (0, 0))
    new_sub, new_root, gram = pl.pallas_call(
        finish,
        grid=(NF // STEP,),
        out_shape=(
            jax.ShapeDtypeStruct((N, SH), F32),
            jax.ShapeDtypeStruct((RR, N), F32),
            jax.ShapeDtypeStruct((N, NB), F32),
        ),
        in_specs=[
            whole,
            root,
            pl.BlockSpec((STEP, NY, N // NY, NBS), lambda i: (i, 0, 0, 0)),
            pl.BlockSpec((SH, STEP * NBS), lambda i: (0, i)),
            pl.BlockSpec((RR, STEP * NBS), lambda i: (0, i)),
        ],
        out_specs=(whole, root, pl.BlockSpec((N, STEP * NBS), lambda i: (0, i))),
    )(xs, xr, low, basis_sub, basis_root)
    return new_sub.T, new_root, gram.T


def solution(mesh):
    placed = (
        P(("leaf", "front"), None),
        P(("leaf", "front"), None),
        P("leaf", "front", None),
        P("leaf", None, "front"),
        P("leaf", None),
        P(("leaf", "front"), None),
        P(("leaf", "front")),
        P(("leaf", "front")),
        P(("leaf", "front"), None, None),
        P(("leaf", "front"), None),
        P(("leaf", "front"), None),
    )
    return jax.shard_map(
        body,
        mesh=mesh,
        in_specs=placed,
        out_specs=(P(("leaf", "front"), None), P(("leaf", "front"), None), P()),
        check_vma=False,
    )
```

```python
import jax
import jax.numpy as jnp
from jax import lax
from jax.experimental import pallas as pl
from jax.experimental.pallas import tpu as pltpu
from jax.sharding import PartitionSpec as P

BF = jnp.bfloat16
F32 = jnp.float32
MESH = pl.DeviceIdType.MESH

N = 64
NF = 8
NY = 4
NZ = 8
NX = 4
NC = 2
NG = NY * NZ
NS = 4
NR = NY * NS
SH = 512
SUB = NF * SH
UP = 2048
UPS = UP // NF
RR = 48
GR = NF * RR
SL = NY * GR
ROOT = NF * SL
RIM = 256
NB = 2048
NBS = NB // NF
PAD = 128
STEP = 8
ORDER = (4, 5, 3, 2, 6, 7, 1)
SENDS = 72
RECVS = 46


def dot(a, b):
    return jnp.dot(a, b, preferred_element_type=F32)


def dot_t(a, b):
    return lax.dot_general(a, b, (((1,), (1,)), ((), ())), preferred_element_type=F32)


def kernel(
    rhs_hbm,
    rroot_hbm,
    factor_hbm,
    coupling_hbm,
    rows_hbm,
    froot_hbm,
    mass_hbm,
    mroot_hbm,
    iface_hbm,
    basis_hbm,
    broot_hbm,
    xs_hbm,
    xr_hbm,
    g_hbm,
    rhs_in,
    rroot_in,
    fac,
    cpl,
    rows_ref,
    frs,
    mass_ref,
    mroot_in,
    iface_ref,
    bas,
    brt,
    onehot,
    frt,
    rhs_all,
    rr_send,
    rr_all,
    rr_sum,
    y_acc,
    up_send,
    up_recv,
    up_all,
    d_send,
    d_recv,
    d_all,
    yr_send,
    yr_sib,
    yr_all,
    x_send,
    x_recv,
    x_all,
    x_sum,
    xr_send,
    xr_recv,
    pk_send,
    pk_recv,
    pk_all,
    xb_send,
    xb_recv,
    xs_send,
    xs_recv,
    xs_acc,
    xr_out,
    if_send,
    if_recv,
    gc_send,
    gc_recv,
    gc_own,
    gp_send,
    gp_recv,
    gz_all,
    g_all,
    ssem,
    rsem,
    lsem,
):
    g = lax.axis_index("leaf")
    f = lax.axis_index("front")
    z = lax.div(g, NY)
    y = lax.rem(g, NY)
    x = lax.div(f, NC)
    c = lax.rem(f, NC)
    other = 1 - c

    def slice_of(i):
        half = lax.div(i, NC)
        return jnp.where(lax.rem(i, NC) == 0, half, NF - 1 - half)

    def holder_of(i):
        return jnp.where(i < NX, NC * i, NC * (NF - 1 - i) + 1)

    part = slice_of(f)
    reached = z >= part

    def dev_f(i):
        return (g, i)

    def dev_x(i):
        return (g, i * NC + c)

    def dev_z(i):
        return (i * NY + y, f)

    def dev_xy(i, j):
        return (z * NY + j, i * NC + c)

    def turn(a, k, n):
        return lax.rem(a + k, n)

    loads = [
        (rhs_hbm, rhs_in),
        (rroot_hbm, rroot_in),
        (rows_hbm, rows_ref),
        (factor_hbm, fac),
        (froot_hbm, frs),
        (coupling_hbm, cpl),
        (iface_hbm, iface_ref),
        (mass_hbm, mass_ref),
        (mroot_hbm, mroot_in),
        (broot_hbm, brt),
        (basis_hbm, bas),
    ]
    loads = [pltpu.make_async_copy(a, b, lsem.at[i]) for i, (a, b) in enumerate(loads)]
    (
        load_rhs,
        load_rroot,
        load_rows,
        load_fac,
        load_frs,
        load_cpl,
        load_iface,
        load_mass,
        load_mroot,
        load_brt,
        load_bas,
    ) = loads
    barrier = pltpu.get_barrier_semaphore()
    def hops(k, n):
        return min(k, n - k)

    peers = [(hops(i, NX), (g, turn(x, i, NX) * NC + c)) for i in range(1, NX)]
    peers += [(hops(i, NX), (g, turn(x, i, NX) * NC + other)) for i in range(NX)]
    peers += [
        (hops(j, NY) + hops(i, NZ), (turn(z, i, NZ) * NY + turn(y, j, NY), f))
        for i in range(NZ)
        for j in range(NY)
        if i or j
    ]
    peers += [
        (hops(i, NX) + hops(j, NY), dev_xy(turn(x, i, NX), turn(y, j, NY)))
        for i in range(1, NX)
        for j in range(1, NY)
    ]
    for _, dev in sorted(peers, key=lambda peer: -peer[0]):
        pl.semaphore_signal(barrier, inc=1, device_id=dev, device_id_type=MESH)
    for load in loads:
        load.start()

    sends = []
    later = []
    slots = [0]
    free = list(range(SENDS))

    def take(n):
        slots[0] += n
        assert slots[0] <= RECVS
        return slots[0] - n

    def push(src, dst, slot, dev, cond=None, to=sends):
        sem = free.pop(0)
        copy = pltpu.make_async_remote_copy(
            src_ref=src,
            dst_ref=dst,
            send_sem=ssem.at[sem],
            recv_sem=rsem.at[slot],
            device_id=dev,
            device_id_type=MESH,
        )
        if cond is None:
            copy.start()
        else:
            pl.when(cond)(copy.start)
        to.append((copy, cond, sem))

    def settle(keep, of=sends):
        done = of[: len(of) - keep]
        del of[: len(of) - keep]
        while done:
            cond = done[0][1]
            same = [copy for copy, other_cond, _ in done if other_cond is cond]
            free.extend(sem for _, other_cond, sem in done if other_cond is cond)
            done = [entry for entry in done if entry[1] is not cond]

            def wait(same=same):
                for copy in same:
                    copy.wait_send()

            if cond is None:
                wait()
            else:
                pl.when(cond)(wait)

    def land(buf, slot):
        pltpu.make_async_remote_copy(
            src_ref=buf,
            dst_ref=buf,
            send_sem=ssem.at[0],
            recv_sem=rsem.at[slot],
            device_id=(g, f),
            device_id_type=MESH,
        ).wait_recv()

    def land_others(buf, slot):
        land(buf.at[pl.ds(0, buf.shape[0] - 1)], slot)

    spot = lax.broadcasted_iota(jnp.int32, (PAD, GR), 0)
    lane = lax.broadcasted_iota(jnp.int32, (PAD, GR), 1)

    def place(j):
        return jnp.where((lane == spot + j * RR) & (spot < RR), 1.0, 0.0).astype(BF)

    widen = jnp.where(
        lax.broadcasted_iota(jnp.int32, (RR, PAD), 0)
        == lax.broadcasted_iota(jnp.int32, (RR, PAD), 1),
        1.0,
        0.0,
    ).astype(BF)
    unit = jnp.where(
        lax.broadcasted_iota(jnp.int32, (N, N), 0) == lax.broadcasted_iota(jnp.int32, (N, N), 1),
        1.0,
        0.0,
    ).astype(BF)
    load_rhs.wait()
    rhs_all[f] = rhs_in[...].astype(BF)
    load_rroot.wait()
    rr_mine = dot(dot_t(unit, rroot_in[...].astype(BF)).astype(BF), widen).astype(BF)
    rr_send[...] = rr_mine
    rr_all[f] = rr_mine

    pl.semaphore_wait(barrier, len(peers))

    at = take(NF)
    for k in range(1, NF):
        push(rhs_all.at[f], rhs_all.at[f], at + f, dev_f(turn(f, k, NF)), f + k < NF)
    at_rhs = at
    at_rr = take(1)
    push(rr_send, rr_all.at[f], at_rr, dev_f(holder_of(z)), part != z)

    load_rows.wait()

    def hot(i, _):
        rows = pl.ds(pl.multiple_of(i * 64, 64), 64)
        ids = lax.broadcasted_iota(jnp.int32, (64, UP), 0) + (part * SL + i * 64)
        onehot[rows, :] = jnp.where(ids == rows_ref[...], 1.0, 0.0).astype(BF)
        return 0

    lax.fori_loop(0, SL // 64, hot, 0)

    load_fac.wait()
    mine = pl.ds(pl.multiple_of(f * SH, 128), SH)
    below = lax.broadcasted_iota(jnp.int32, (SH, SH), 1) <= lax.broadcasted_iota(
        jnp.int32, (SH, SH), 0
    )
    diag = jnp.where(below, fac[:, mine].astype(F32), 0.0).astype(BF)
    fac[:, mine] = diag
    y_acc[...] = dot_t(rhs_all[f], diag)

    load_frs.wait()

    def lower(j, _):
        cols = pl.ds(pl.multiple_of(j * SL, 128), SL)
        row_ids = lax.broadcasted_iota(jnp.int32, (RR, SL), 0) + (g * GR + f * RR)
        col_ids = lax.broadcasted_iota(jnp.int32, (RR, SL), 1) + j * SL
        frs[:, cols] = jnp.where(col_ids <= row_ids, frs[:, cols].astype(F32), 0.0).astype(BF)
        return 0

    lax.fori_loop(0, NF, lower, 0)
    for k in range(1, NF):

        @pl.when(f >= k)
        def _(k=k):
            p = f - k
            land(rhs_all.at[p], at_rhs + p)
            cols = pl.ds(pl.multiple_of(p * SH, 128), SH)
            y_acc[...] += dot_t(rhs_all[p], fac[:, cols])

    y_low = y_acc[...].astype(BF)

    load_cpl.wait()
    at = take(1)
    for k in ORDER + (0,):
        p = turn(f, k, NF)
        rows = pl.ds(pl.multiple_of(p * UPS, 128), UPS)
        piece = dot_t(y_low, cpl[rows, :]).astype(BF)
        if k:
            up_send[k] = piece
            push(up_send.at[k], up_recv.at[f], at, dev_f(p))
        else:
            up_recv[f] = piece
    settle(NF - 1)

    @pl.when(part == z)
    def _():
        land_others(rr_all, at_rr)
        rr_sum[...] = sum(dot(rr_all[j], place(j)) for j in range(NF))

    @pl.when(part != z)
    def _():
        rr_sum[...] = jnp.zeros_like(rr_sum)

    land_others(up_recv, at)
    up_all[f] = sum(up_recv[j].astype(F32) for j in range(NF)).astype(BF)
    at = take(1)
    for k in ORDER:
        push(up_all.at[f], up_all.at[f], at, dev_f(turn(f, k, NF)))

    land_others(up_all, at)

    at_frt = take(1)
    my_rows = pl.ds(pl.multiple_of(f * RR, 16), RR)
    for k in range(1, NF):
        p = turn(f, k, NF)
        to = slice_of(p)
        cols = pl.ds(pl.multiple_of(to * SL, 128), SL)
        push(frs.at[:, cols], frt.at[my_rows], at_frt, dev_f(p), to <= z, later)
    frt[my_rows, :] = frs[:, pl.ds(pl.multiple_of(part * SL, 128), SL)]

    adds = lax.rem(z + y + c, 2) == 0
    spot_mine = 2 * z + lax.div(y, 2)

    def cut(chunk, q, send):
        send[q] = chunk(q).astype(BF).reshape(NS, N // NS, GR)

    def hand_out(q, send, recv, slot_of, at, cond=None):
        for i in range(NS):
            zi = 2 * q + i // 2
            to = zi * NY + 2 * (i % 2) + lax.rem(zi + c, 2)
            use = to != g if cond is None else cond & (to != g)
            push(send.at[q, i], recv.at[slot_of(to)], at, (to, f), use)

    def own_piece(send):
        return send[lax.div(spot_mine, NS), lax.rem(spot_mine, NS)]

    def hand_back(full, some):
        at = take(1)
        for k in sorted(range(1, NG), key=lambda k: -min(k, NG - k)):
            to = turn(g, k, NG)
            use = adds & (lax.div(to, NY) >= part) if some else adds
            push(full.at[spot_mine], full.at[spot_mine], at, (to, f), use)
        wanted = reached if some else part >= 0

        @pl.when(adds & wanted)
        def _():
            land(full.at[pl.ds(0, NR - 1)], at)

        @pl.when(jnp.logical_not(adds) & wanted)
        def _():
            land(full, at)

        parts = [full[pl.ds(NS * j, NS)].reshape(N, GR) for j in range(NY)]
        return jnp.concatenate(parts, axis=1)

    up_low = jnp.concatenate([up_all[j] for j in range(NF)], axis=1)

    def scatter_chunk(q):
        total = dot_t(up_low, onehot[pl.ds(pl.multiple_of(q * GR, 128), GR), :])
        return jnp.where(q == y, rr_sum[...], 0.0) - total

    at = take(1)
    for k in (2, 1, 3, 0):
        q = turn(lax.div(z, 2), k, NY)
        cut(scatter_chunk, q, d_send)
        hand_out(q, d_send, d_recv, lambda to: lax.rem(g - to + NG - 1, NG), at)
    settle(NR)

    @pl.when(adds)
    def _():
        land(d_recv.at[pl.ds(0, NG - 1)], at)
        total = own_piece(d_send).astype(F32)
        for j in range(NG - 1):
            total += d_recv[j].astype(F32)
        d_all[spot_mine] = total.astype(BF)

    b_low = hand_back(d_all, True)

    @pl.when(reached)
    def _():
        land(frt.at[pl.ds(0, GR - RR)], at_frt)
        yr_send[...] = dot_t(b_low, frt[...]).astype(BF)

    @pl.when(jnp.logical_not(reached))
    def _():
        yr_send[...] = jnp.zeros_like(yr_send)

    at = take(1)
    push(yr_send, yr_sib, at, dev_f(x * NC + other))
    land(yr_sib, at)
    yr_all[x] = (yr_send[...].astype(F32) + yr_sib[...].astype(F32)).astype(BF)
    at = take(1)
    for k in (2, 1, 3):
        push(yr_all.at[x], yr_all.at[x], at, dev_x(turn(x, k, NX)))
    settle(NX - 1)
    land_others(yr_all, at)
    yr_low = sum(yr_all[j].astype(F32) for j in range(NX)).astype(BF)

    def back_chunk(q):
        return dot(yr_low, frt[:, pl.ds(pl.multiple_of(q * GR, 128), GR)])

    at = take(NZ)
    for k in (2, 1, 3, 0):
        q = turn(lax.div(z, 2), k, NY)

        @pl.when(reached)
        def _(q=q):
            cut(back_chunk, q, x_send)

        hand_out(q, x_send, x_recv, lambda to: g, at + z, reached)
    settle(NR)

    @pl.when(adds)
    def _():
        x_sum[...] = jnp.zeros_like(x_sum)

        @pl.when(reached)
        def _():
            x_recv[g] = own_piece(x_send)

        for i in range(NZ):

            @pl.when(i >= part)
            def _(i=i):
                @pl.when(z == i)
                def _():
                    land(x_recv.at[pl.ds(NY * i, NY - 1)], at + i)

                @pl.when(z != i)
                def _():
                    land(x_recv.at[pl.ds(NY * i, NY)], at + i)

                x_sum[...] += sum(x_recv[NY * i + j].astype(F32) for j in range(NY))

        x_all[spot_mine] = x_sum[...].astype(BF)

    x_low = hand_back(x_all, False)

    at = take(1)
    for k in ORDER + (0,):
        p = turn(f, k, NF)
        cols = pl.ds(pl.multiple_of(p * UPS, 128), UPS)
        piece = dot(x_low, onehot[:, cols]).astype(BF)
        if k:
            pk_send[k] = piece
            push(pk_send.at[k], pk_recv.at[f], at, dev_f(p))
        else:
            pk_recv[f] = piece
    at_xr = take(1)

    @pl.when(part == z)
    def _():
        block = x_all[pl.ds(pl.multiple_of(NS * y, NS), NS)].reshape(N, GR)
        for j in range(NF):
            xr_send[j] = dot_t(block, place(j)).astype(BF)
        xr_recv[...] = xr_send[f]

    for k in ORDER:
        p = turn(f, k, NF)
        push(xr_send.at[p], xr_recv, at_xr, dev_f(p), part == z)
    settle(2 * NF - 2)
    settle(0, later)
    land_others(pk_recv, at)
    pk_all[f] = sum(pk_recv[j].astype(F32) for j in range(NF)).astype(BF)
    at = take(1)
    for k in ORDER:
        push(pk_all.at[f], pk_all.at[f], at, dev_f(turn(f, k, NF)))
    for k in (0,) + ORDER[::-1]:
        p = turn(f, NF - k, NF)
        if k == ORDER[-1]:
            land_others(pk_all, at)
        rows = pl.ds(pl.multiple_of(p * UPS, 128), UPS)
        y_acc[...] -= dot(pk_all[p], cpl[rows, :])
    t_low = y_acc[...].astype(BF)

    at = take(NX)
    for k in range(NX):
        used = (x >= k) if k else (c == 1)
        i = turn(x, NX - k, NX)

        @pl.when(used)
        def _(i=i):
            cols = pl.ds(pl.multiple_of((i * NC + other) * SH, 128), SH)
            xb_send[i] = dot(t_low, fac[:, cols]).astype(BF)

        push(xb_send.at[i], xb_recv.at[i], at + i, dev_f(x * NC + other), used)
    at_xs = take(NX)
    for k in (1, 2, 3, 0):
        used = x >= k
        i = turn(x, NX - k, NX)
        cols = pl.ds(pl.multiple_of((i * NC + c) * SH, 128), SH)
        if k:

            @pl.when(used)
            def _(i=i, cols=cols):
                part = dot(t_low, fac[:, cols])
                land(xb_recv.at[i], at + i)
                xs_send[i] = (part + xb_recv[i].astype(F32)).astype(BF)

            push(xs_send.at[i], xs_recv.at[x], at_xs + x, dev_x(i), used)
        else:
            xs_acc[...] = dot(t_low, fac[:, cols])

            @pl.when(c == 0)
            def _(i=i):
                land(xb_recv.at[i], at + i)
                xs_acc[...] += xb_recv[i].astype(F32)

    for k in range(1, NX):

        @pl.when(x + k < NX)
        def _(k=k):
            land(xs_recv.at[x + k], at_xs + x + k)
            xs_acc[...] += xs_recv[x + k].astype(F32)

    at_next = take(1)
    at_prev = take(1)
    xs_low = xs_acc[...].astype(BF)
    keep_sub = pltpu.make_async_copy(xs_acc, xs_hbm, lsem.at[11])
    keep_sub.start()
    if_send[0] = xs_low[:, SH - RIM :]
    push(if_send.at[0], if_recv.at[0], at_next, (turn(g, 1, NG), f))
    load_iface.wait()
    if_send[1] = dot(xs_low[:, :RIM], iface_ref[...]).astype(BF)
    push(if_send.at[1], if_recv.at[1], at_prev, (turn(g, NG - 1, NG), f))

    settle(2)

    @pl.when(part != z)
    def _():
        land(xr_recv, at_xr)

    load_mroot.wait()
    xr_out[...] = dot_t(widen, xr_recv[...])
    keep_root = pltpu.make_async_copy(xr_out, xr_hbm, lsem.at[12])
    keep_root.start()
    mx_own = (xr_recv[...].astype(F32)[:, :RR] * mroot_in[...]).astype(BF)
    load_brt.wait()

    load_mass.wait()
    mass_x = xs_acc[...] * mass_ref[...]
    land(if_recv.at[0], at_next)
    first = mass_x[:, :RIM] + dot_t(if_recv[0], iface_ref[...])
    land(if_recv.at[1], at_prev)
    last = mass_x[:, SH - RIM :] + if_recv[1].astype(F32)
    mx = jnp.concatenate([first, last], axis=1).astype(BF)

    load_bas.wait()

    def gram_part(block):
        cols = pl.ds(pl.multiple_of(block * NBS, 128), NBS)
        return dot(mx, bas[:, cols]) + dot(mx_own, brt[:, cols])

    at = take(NX)
    for j in range(NX):
        gc_send[j] = gram_part(other * NX + j).astype(BF)
        push(gc_send.at[j], gc_recv.at[j], at + j, dev_f(x * NC + other))
    for j in range(NX):
        gc_own[j] = gram_part(c * NX + j)
    at_p = take(1)
    for i in (2, 1, 3, 0):
        xi = turn(x, i, NX)
        land(gc_recv.at[xi], at + xi)
        pair = gc_own[xi] + gc_recv[xi].astype(F32)
        gp_send[xi] = pair.astype(BF).reshape(NY, N // NY, NBS)
        for j in (2, 1, 3, 0):
            if i or j:
                yj = turn(y, j, NY)
                slot = ((NX - i) % NX) * NY + (NY - j) % NY - 1
                push(gp_send.at[xi, yj], gp_recv.at[slot], at_p, dev_xy(xi, yj))
    settle(NX * NY - 1)
    land(gp_recv, at_p)
    total = gp_send[x, y].astype(F32)
    for j in range(NX * NY - 1):
        total += gp_recv[j].astype(F32)
    gz_all[z] = total.astype(BF)
    at = take(1)
    for k in (4, 3, 5, 2, 6, 1, 7):
        push(gz_all.at[z], gz_all.at[z], at, dev_z(turn(z, k, NZ)))
    settle(NZ - 1)
    land_others(gz_all, at)
    mine = c * NX + x
    g_all[mine, y] = sum(gz_all[j].astype(F32) for j in range(NZ)).astype(BF)
    at = take(1)
    for i in (2, 1, 3, 0):
        for j in (2, 1, 3, 0):
            if i or j:
                to = dev_xy(turn(x, i, NX), turn(y, j, NY))
                push(g_all.at[mine, y], g_all.at[mine, y], at, to)
    settle(NX * NY - 1)
    land(gp_recv, at)
    at = take(1)
    half = pl.ds(pl.multiple_of(c * NX, NX), NX)
    push(g_all.at[half], g_all.at[half], at, dev_f(x * NC + other))

    keep_mine = pltpu.make_async_copy(g_all.at[half], g_hbm.at[half], lsem.at[13])
    keep_mine.start()
    settle(1)
    rest = pl.ds(pl.multiple_of(other * NX, NX), NX)
    land(g_all.at[rest], at)
    keep_rest = pltpu.make_async_copy(g_all.at[rest], g_hbm.at[rest], lsem.at[14])
    keep_rest.start()

    settle(0)
    for keep in (keep_sub, keep_root, keep_mine, keep_rest):
        keep.wait()


def finish(xs_ref, xr_ref, g_ref, bas_ref, brt_ref, new_sub_ref, new_root_ref, gram_ref):
    @pl.when(pl.program_id(0) == 0)
    def _():
        new_sub_ref[...] = xs_ref[...]
        new_root_ref[...] = xr_ref[...]

    for j in range(STEP):
        cols = pl.ds(j * NBS, NBS)
        low = g_ref[j].reshape(N, NBS)
        gram_ref[:, cols] = low.astype(F32)
        new_sub_ref[...] -= dot_t(low, bas_ref[:, cols])
        new_root_ref[...] -= dot_t(brt_ref[:, cols], low)


def body(
    rhs_sub,
    rhs_root,
    factor_sub,
    coupling,
    update_rows,
    factor_root,
    mass_sub,
    mass_root,
    interface,
    basis_sub,
    basis_root,
):
    hbm = pl.BlockSpec(memory_space=pl.ANY)
    leaf_sum = [
        pltpu.VMEM((NY, NS, N // NS, GR), BF),
        pltpu.VMEM((NG, N // NS, GR), BF),
        pltpu.VMEM((NR, N // NS, GR), BF),
    ]
    xs, xr, low = pl.pallas_call(
        kernel,
        out_shape=(
            jax.ShapeDtypeStruct((N, SH), F32),
            jax.ShapeDtypeStruct((RR, N), F32),
            jax.ShapeDtypeStruct((NF, NY, N // NY, NBS), BF),
        ),
        in_specs=[hbm] * 11,
        out_specs=(hbm, hbm, hbm),
        scratch_shapes=[
            pltpu.VMEM((N, SH), F32),
            pltpu.VMEM((RR, N), F32),
            pltpu.VMEM((SH, SUB), BF),
            pltpu.VMEM((UP, SH), BF),
            pltpu.VMEM((1, UP), jnp.int32),
            pltpu.VMEM((RR, ROOT), BF),
            pltpu.VMEM((1, SH), F32),
            pltpu.VMEM((1, RR), F32),
            pltpu.VMEM((RIM, RIM), BF),
            pltpu.VMEM((SH, NB), BF),
            pltpu.VMEM((RR, NB), BF),
            pltpu.VMEM((SL, UP), BF),
            pltpu.VMEM((GR, SL), BF),
            pltpu.VMEM((NF, N, SH), BF),
            pltpu.VMEM((N, PAD), BF),
            pltpu.VMEM((NF, N, PAD), BF),
            pltpu.VMEM((N, GR), F32),
            pltpu.VMEM((N, SH), F32),
            pltpu.VMEM((NF, N, UPS), BF),
            pltpu.VMEM((NF, N, UPS), BF),
            pltpu.VMEM((NF, N, UPS), BF),
            *leaf_sum,
            pltpu.VMEM((N, GR), BF),
            pltpu.VMEM((N, GR), BF),
            pltpu.VMEM((NX, N, GR), BF),
            *leaf_sum,
            pltpu.VMEM((N // NS, GR), F32),
            pltpu.VMEM((NF, N, PAD), BF),
            pltpu.VMEM((N, PAD), BF),
            pltpu.VMEM((NF, N, UPS), BF),
            pltpu.VMEM((NF, N, UPS), BF),
            pltpu.VMEM((NF, N, UPS), BF),
            pltpu.VMEM((NX, N, SH), BF),
            pltpu.VMEM((NX, N, SH), BF),
            pltpu.VMEM((NX, N, SH), BF),
            pltpu.VMEM((NX, N, SH), BF),
            pltpu.VMEM((N, SH), F32),
            pltpu.VMEM((RR, N), F32),
            pltpu.VMEM((2, N, RIM), BF),
            pltpu.VMEM((2, N, RIM), BF),
            pltpu.VMEM((NX, N, NBS), BF),
            pltpu.VMEM((NX, N, NBS), BF),
            pltpu.VMEM((NX, N, NBS), F32),
            pltpu.VMEM((NX, NY, N // NY, NBS), BF),
            pltpu.VMEM((NX * NY - 1, N // NY, NBS), BF),
            pltpu.VMEM((NZ, N // NY, NBS), BF),
            pltpu.VMEM((NF, NY, N // NY, NBS), BF),
            pltpu.SemaphoreType.DMA((SENDS,)),
            pltpu.SemaphoreType.DMA((RECVS,)),
            pltpu.SemaphoreType.DMA((15,)),
        ],
        compiler_params=pltpu.CompilerParams(
            collective_id=0, has_side_effects=True, vmem_limit_bytes=56 * 1024 * 1024
        ),
    )(
        rhs_sub.T,
        rhs_root,
        factor_sub[0],
        coupling[0],
        update_rows,
        factor_root,
        mass_sub[None, :],
        mass_root[None, :],
        interface[0],
        basis_sub,
        basis_root,
    )
    whole = pl.BlockSpec((N, SH), lambda i: (0, 0))
    root = pl.BlockSpec((RR, N), lambda i: (0, 0))
    new_sub, new_root, gram = pl.pallas_call(
        finish,
        grid=(NF // STEP,),
        out_shape=(
            jax.ShapeDtypeStruct((N, SH), F32),
            jax.ShapeDtypeStruct((RR, N), F32),
            jax.ShapeDtypeStruct((N, NB), F32),
        ),
        in_specs=[
            whole,
            root,
            pl.BlockSpec((STEP, NY, N // NY, NBS), lambda i: (i, 0, 0, 0)),
            pl.BlockSpec((SH, STEP * NBS), lambda i: (0, i)),
            pl.BlockSpec((RR, STEP * NBS), lambda i: (0, i)),
        ],
        out_specs=(whole, root, pl.BlockSpec((N, STEP * NBS), lambda i: (0, i))),
    )(xs, xr, low, basis_sub, basis_root)
    return new_sub.T, new_root, gram.T


def solution(mesh):
    placed = (
        P(("leaf", "front"), None),
        P(("leaf", "front"), None),
        P("leaf", "front", None),
        P("leaf", None, "front"),
        P("leaf", None),
        P(("leaf", "front"), None),
        P(("leaf", "front")),
        P(("leaf", "front")),
        P(("leaf", "front"), None, None),
        P(("leaf", "front"), None),
        P(("leaf", "front"), None),
    )
    return jax.shard_map(
        body,
        mesh=mesh,
        in_specs=placed,
        out_specs=(P(("leaf", "front"), None), P(("leaf", "front"), None), P()),
        check_vma=False,
    )
```
